128 devices in a mesh: dp: 2 (over core), seq: 64 (over z, x, y).
Axes of the slice: x: 4, y: 4, z: 4, core: 2. Of those that a mesh axis runs over, the one named last changes fastest.
Arguments:
- queries: bfloat16 [512, 64, 2048], P(('dp', 'seq'))
- outputs: bfloat16 [512, 64, 2048], P(('dp', 'seq')), may hold values from -6 to 6
- out_grad: bfloat16 [512, 64, 2048], P(('dp', 'seq')), may hold values from -6 to 6
- keys: bfloat16 [512, 128, 2048], P(('dp', 'seq'))
- values: bfloat16 [512, 128, 2048], P(('dp', 'seq')), may hold values from -6 to 6
- owner: int32 [512, 2], P(('dp', 'seq')), may hold values from 0 to 63, as said below
- slot: int32 [512, 2], P(('dp', 'seq')), may hold values from 0 to 3
- pos_bias: float32 [1024, 128], replicated, may hold values from -6 to 6
Outputs:
- query_grad: bfloat16 [512, 64, 2048], P(('dp', 'seq'))
- key_grad: float32 [512, 128, 2048], P(('dp', 'seq'))
- value_grad: float32 [512, 128, 2048], P(('dp', 'seq'))
- bias_grad: float32 [1024, 128], P(('dp', 'seq'))
The draws below stay inside these ranges and needn't reach their ends.
Inputs may be any that keep to these rules, and one draw needn't show every extreme that they name: A neighbour's owner is at most 2 positions away, cyclically along seq, from the device that holds the span. From the spans of one device at most 2 neighbours have the same owner, and in every draw some owner receives exactly 2 from some device.
All inputs are finite; a program needn't handle non-finite values.
Results may differ from the reference program's by a relative error of at most 0.0048.
Values may be sent and summed in bfloat16 or wider, within the bound.
A program may use at most 192 MiB of HBM per device.

```python
import jax
import jax.numpy as jnp
from jax import lax

HEADS = 16
HEAD_DIM = 128
SPAN = 64
NB_LEN = 128
REACH = 2
CH_DEV = 4
HD = 2048
NB_DEV = 4
CAP = 2
SPANS = 512
BLOCKS = 512
N_SEQ = 64


def draw_queries(key, part):
    key = jax.random.fold_in(key, 1)
    shape = (SPANS, SPAN, HEADS, HEAD_DIM)
    noise = jax.random.normal(key, shape, dtype=jnp.float32)
    return noise.reshape(SPANS, SPAN, HD).astype(jnp.bfloat16)


def draw_keys(key, part):
    key = jax.random.fold_in(key, 2)
    shape = (BLOCKS, NB_LEN, HEADS, HEAD_DIM)
    noise = jax.random.normal(key, shape, dtype=jnp.float32)
    return noise.reshape(BLOCKS, NB_LEN, HD).astype(jnp.bfloat16)


def draw_owner(key, part):
    key = jax.random.fold_in(key, 3)
    lane_total = (2 * REACH + 1) * CAP
    device_total = SPANS // CH_DEV
    orders = jax.vmap(lambda single: jax.random.permutation(single, lane_total))(jax.random.split(key, device_total))
    picked = orders[:, :2 * CH_DEV]
    offsets = picked // CAP - REACH
    seats = jnp.arange(device_total, dtype=jnp.int32) % N_SEQ
    owners = (seats[:, None] + offsets) % N_SEQ
    return owners.reshape(SPANS, 2).astype(jnp.int32)


def place_ends(entries, key, smallest, top_value):
    index_at = [jax.random.randint(jax.random.fold_in(key, axis), (), 0, length) for axis, length in enumerate(entries.shape)]
    longest = entries.shape.index(max(entries.shape))
    next_to = index_at[:longest] + [(index_at[longest] + 1) % entries.shape[longest]] + index_at[longest + 1:]
    return entries.at[tuple(index_at)].set(smallest).at[tuple(next_to)].set(top_value)


def block_scale(rng, dims, cuts, least, largest):
    level = 1.0
    for axis_at, shards_of in cuts:
        heights = jax.random.uniform(jax.random.fold_in(jax.random.fold_in(rng, 6), axis_at), (shards_of,), jnp.float32, least / len(cuts), largest / len(cuts))
        level = level * jnp.repeat(jnp.exp(heights), dims[axis_at] // shards_of).reshape((-1,) + (1,) * (len(dims) - 1 - axis_at))
    return level


def scatter_about(own_key, extent, width, most, pieces=(), held_as=jnp.bfloat16):
    gain = block_scale(own_key, extent, pieces, -0.22, 0.18) if pieces else 1.0
    result = jax.random.normal(own_key, extent, jnp.float32) * width * gain
    return jnp.minimum(jnp.maximum(result, -most), most).astype(held_as)


def setup_inputs(seed: int = 0) -> dict:
    key_list = jax.random.split(jax.random.key(seed), 9)
    return {
        "queries": draw_queries(jax.random.fold_in(key_list[8], 71), 0),
        "outputs": scatter_about(key_list[1], (SPANS, SPAN, HD), 1.0, 6.0, ((0, 128),)),
        "out_grad": scatter_about(key_list[2], (SPANS, SPAN, HD), 1.0, 6.0, ((0, 128),)),
        "keys": draw_keys(jax.random.fold_in(key_list[8], 71), 0),
        "values": scatter_about(key_list[4], (BLOCKS, NB_LEN, HD), 1.0, 6.0, ((0, 128),)),
        "owner": draw_owner(jax.random.fold_in(key_list[8], 71), 0),
        "slot": place_ends(jax.random.randint(key_list[6], (SPANS, 2), 0, NB_DEV), jax.random.fold_in(key_list[6], 1), 0, NB_DEV - 1).astype(jnp.int32),
        "pos_bias": scatter_about(key_list[7], (HEADS * SPAN, NB_LEN), 1.0, 6.0, (), jnp.float32),
    }


def span_backward(query_rows, output_rows, grad_rows, key_rows, value_rows, bias_pair):
    scaling = HEAD_DIM ** -0.5
    query_heads = query_rows.astype(jnp.float32).reshape(SPAN, HEADS, HEAD_DIM)
    output_heads = output_rows.astype(jnp.float32).reshape(SPAN, HEADS, HEAD_DIM)
    grad_heads = grad_rows.astype(jnp.float32).reshape(SPAN, HEADS, HEAD_DIM)
    key_heads = key_rows.astype(jnp.float32).reshape(2 * NB_LEN, HEADS, HEAD_DIM)
    value_heads = value_rows.astype(jnp.float32).reshape(2 * NB_LEN, HEADS, HEAD_DIM)
    scores = jnp.einsum("ihd,jhd->hij", query_heads, key_heads) * scaling + bias_pair
    highest = jnp.max(scores, axis=-1, keepdims=True)
    log_total = highest[..., 0] + jnp.log(jnp.sum(jnp.exp(scores - highest), axis=-1))
    weights = jnp.exp(scores - log_total[..., None])
    weights_low = lax.optimization_barrier(weights.astype(jnp.bfloat16)).astype(jnp.float32)
    row_terms = jnp.transpose(jnp.sum(grad_heads * output_heads, axis=-1), (1, 0))
    grad_weights = jnp.einsum("ihd,jhd->hij", grad_heads, value_heads)
    grad_scores = weights * (grad_weights - row_terms[..., None])
    grad_low = lax.optimization_barrier(grad_scores.astype(jnp.bfloat16)).astype(jnp.float32)
    query_grad = (jnp.einsum("hij,jhd->ihd", grad_low, key_heads) * scaling).reshape(SPAN, HD)
    key_grad = (jnp.einsum("hij,ihd->jhd", grad_low, query_heads) * scaling).reshape(2 * NB_LEN, HD)
    value_grad = jnp.einsum("hij,ihd->jhd", weights_low, grad_heads).reshape(2 * NB_LEN, HD)
    bias_grad = jnp.sum(grad_scores.reshape(HEADS, SPAN, 2, NB_LEN), axis=2)
    return query_grad.astype(jnp.bfloat16), key_grad, value_grad, bias_grad


def reference(queries, outputs, out_grad, keys, values, owner, slot, pos_bias):
    group_of = (jnp.arange(SPANS, dtype=jnp.int32) // CH_DEV) // N_SEQ
    block_ids = ((group_of[:, None] * N_SEQ + owner) * NB_DEV + slot).astype(jnp.int32)
    bias_three = pos_bias.reshape(HEADS, SPAN, NB_LEN)
    bias_pair = jnp.concatenate([bias_three, bias_three], axis=-1)

    def advance(carry, inputs):
        key_total, value_total, bias_total = carry
        query_rows, output_rows, grad_rows, pair_ids = inputs
        key_rows = jnp.concatenate([keys[pair_ids[0]], keys[pair_ids[1]]], axis=0)
        value_rows = jnp.concatenate([values[pair_ids[0]], values[pair_ids[1]]], axis=0)
        query_grad, key_grad, value_grad, bias_grad = span_backward(query_rows, output_rows, grad_rows, key_rows, value_rows, bias_pair)
        key_total = key_total.at[pair_ids[0]].add(key_grad[:NB_LEN]).at[pair_ids[1]].add(key_grad[NB_LEN:])
        value_total = value_total.at[pair_ids[0]].add(value_grad[:NB_LEN]).at[pair_ids[1]].add(value_grad[NB_LEN:])
        return (key_total, value_total, bias_total + bias_grad), query_grad

    start = (jnp.zeros((BLOCKS, NB_LEN, HD), jnp.float32), jnp.zeros((BLOCKS, NB_LEN, HD), jnp.float32), jnp.zeros((HEADS, SPAN, NB_LEN), jnp.float32))
    (key_total, value_total, bias_total), query_grads = lax.scan(advance, start, (queries, outputs, out_grad, block_ids))
    return query_grads, key_total, value_total, bias_total.reshape(HEADS * SPAN, NB_LEN)
```

```python
import functools

import jax
import jax.numpy as jnp
from jax import lax
from jax.experimental import pallas as pl
from jax.experimental.pallas import tpu as pltpu
from jax.sharding import PartitionSpec as P

REACH = 2
CAP = 2
LANES = 2 * REACH + 1
SLOTS = LANES * CAP
HEADS_PER_PART = 2
AHEAD = 2
UNUSED = 1e30
MESH = pl.DeviceIdType.MESH
REMOTE = tuple(lane for lane in range(LANES) if lane != REACH)


def rows_dot(a, b):
    return lax.dot_general(a, b, (((1,), (1,)), ((), ())), preferred_element_type=jnp.float32)


def plain_dot(a, b):
    return jnp.dot(a, b, preferred_element_type=jnp.float32)


def kernel(
    cfg,
    owner_ref,
    slot_ref,
    q_ref,
    o_ref,
    g_ref,
    k_ref,
    v_ref,
    bias_ref,
    qg_ref,
    kg_ref,
    vg_ref,
    bg_ref,
    meta_send,
    meta_recv,
    mask_row,
    mask_col,
    terms,
    span_send,
    span_recv,
    part_send,
    part_recv,
    part_pick,
    total_send,
    total_recv,
    tops,
    exps,
    grads,
    w_wide,
    d_wide,
    d_tall,
    dq_send,
    dq_recv,
    dq_pick,
    kg_hold,
    vg_hold,
    bias_sum,
    core_recv,
    z_send,
    z_recv,
    x_send,
    x_recv,
    y_send,
    y_recv,
    meta_ss,
    meta_rs,
    span_ss,
    span_rs,
    part_ss,
    part_rs,
    total_ss,
    total_rs,
    dq_ss,
    dq_rs,
    hold_sem,
    core_ss,
    core_rs,
    ring_ss,
    ring_rs,
):
    spans, rows, seq_count, parts, blocks, scaling = cfg
    width = HEADS_PER_PART * 128
    pairs = 2 * spans
    dp = lax.axis_index("dp")
    me = lax.axis_index("seq")
    at_z, at_x, at_y = me // 16, (me // 4) % 4, me % 4

    def owner_at(lane):
        return (dp, lax.rem(me + (lane - REACH) + seq_count, seq_count))

    def asker_at(lane):
        return (dp, lax.rem(me - (lane - REACH) + seq_count, seq_count))

    ring_peers = []
    for step in (1, 2, 3):
        ring_peers.append((dp, ((at_z + step) % 4) * 16 + at_x * 4 + at_y))
        ring_peers.append((dp, at_z * 16 + ((at_x + step) % 4) * 4 + at_y))
        ring_peers.append((dp, at_z * 16 + at_x * 4 + (at_y + step) % 4))
    greeted = [owner_at(lane) for lane in REMOTE] + ring_peers + [(1 - dp, me)]
    barrier = pltpu.get_barrier_semaphore()
    for device in greeted:
        pl.semaphore_signal(barrier, inc=1, device_id=device, device_id_type=MESH)

    lane_of = [
        lax.rem(owner_ref[p // 2, p % 2] - me + REACH + seq_count, seq_count) for p in range(pairs)
    ]
    place = []
    for p in range(pairs):
        rank = jnp.int32(0)
        for other in range(p):
            rank = rank + jnp.where(lane_of[other] == lane_of[p], 1, 0)
        place.append(jnp.minimum(lane_of[p] * CAP + rank, SLOTS - 1))
    chosen, filled, block_id, partner = [], [], [], []
    for s in range(SLOTS):
        pick, used, block, mate = jnp.int32(0), jnp.int32(0), jnp.int32(0), jnp.int32(0)
        for p in range(pairs):
            hit = place[p] == s
            pick = jnp.where(hit, p // 2, pick)
            used = jnp.where(hit, 1, used)
            block = jnp.where(hit, slot_ref[p // 2, p % 2], block)
            mate = jnp.where(hit, place[p ^ 1], mate)
        chosen.append(pick)
        filled.append(used)
        block_id.append(block)
        partner.append((mate // 2) * 2 + (mate + s) % 2)

    lane_id = lax.broadcasted_iota(jnp.int32, (8, 128), 1)
    row_id = lax.broadcasted_iota(jnp.int32, (8, 128), 0)
    first_half = lane_id < rows

    def meta_copy(lane):
        return pltpu.make_async_remote_copy(
            src_ref=meta_send.at[lane],
            dst_ref=meta_recv.at[lane],
            send_sem=meta_ss.at[lane],
            recv_sem=meta_rs.at[lane],
            device_id=owner_at(lane),
            device_id_type=MESH,
        )

    def span_copy(part, lane):
        return pltpu.make_async_remote_copy(
            src_ref=span_send.at[part, lane],
            dst_ref=span_recv.at[part, lane],
            send_sem=span_ss.at[part, lane],
            recv_sem=span_rs.at[part, lane],
            device_id=owner_at(lane),
            device_id_type=MESH,
        )

    def part_copy(part, lane):
        return pltpu.make_async_remote_copy(
            src_ref=part_send.at[part, lane],
            dst_ref=part_recv.at[part, lane],
            send_sem=part_ss.at[part, lane],
            recv_sem=part_rs.at[part, lane],
            device_id=asker_at(lane),
            device_id_type=MESH,
        )

    def total_copy(part, lane):
        return pltpu.make_async_remote_copy(
            src_ref=total_send.at[part, lane],
            dst_ref=total_recv.at[part, lane],
            send_sem=total_ss.at[part, lane],
            recv_sem=total_rs.at[part, lane],
            device_id=owner_at(lane),
            device_id_type=MESH,
        )

    def dq_copy(part, lane):
        return pltpu.make_async_remote_copy(
            src_ref=dq_send.at[part, lane],
            dst_ref=dq_recv.at[part, lane],
            send_sem=dq_ss.at[part, lane],
            recv_sem=dq_rs.at[part, lane],
            device_id=asker_at(lane),
            device_id_type=MESH,
        )

    def hold_copy(part, which):
        held, out = ((kg_hold, kg_ref), (vg_hold, vg_ref))[which]
        columns = pl.ds(pl.multiple_of(part * width, width), width)
        return pltpu.make_async_copy(held.at[part], out.at[:, columns], hold_sem.at[which, part])

    def pack(part):
        columns = pl.ds(pl.multiple_of(part * width, width), width)
        for lane in range(LANES):
            target = span_recv if lane == REACH else span_send
            for half in range(CAP):
                span = chosen[lane * CAP + half]
                target[part, lane, 0, half * rows : (half + 1) * rows, :] = q_ref[span, :, columns]
                target[part, lane, 1, half * rows : (half + 1) * rows, :] = g_ref[span, :, columns]

    def send_spans(part):
        for lane in REMOTE:
            span_copy(part, lane).start()

    for lane in range(LANES):
        tile = jnp.where(first_half, block_id[2 * lane], block_id[2 * lane + 1])
        target = meta_recv if lane == REACH else meta_send
        target[lane] = tile.astype(jnp.float32)
    pack(0)
    pl.semaphore_wait(barrier, len(greeted))
    for lane in REMOTE:
        meta_copy(lane).start()
    send_spans(0)

    def pack_and_send(part, carry):
        pack(part)
        send_spans(part)
        return carry

    lax.fori_loop(1, AHEAD, pack_and_send, 0)

    def span_terms(span, carry):
        wide_lane = lax.broadcasted_iota(jnp.int32, (rows, 128), 1)
        gathered = jnp.zeros((rows, 128), jnp.float32)
        for head in range(parts * HEADS_PER_PART):
            cols = slice(head * 128, (head + 1) * 128)
            product = g_ref[span, :, cols].astype(jnp.float32) * o_ref[span, :, cols].astype(
                jnp.float32
            )
            gathered = jnp.where(
                wide_lane == head, jnp.sum(product, axis=1, keepdims=True), gathered
            )
        turned = jnp.concatenate([gathered, gathered], axis=0).T
        for part in range(parts):
            first = part * HEADS_PER_PART
            terms[span, part, HEADS_PER_PART : 2 * HEADS_PER_PART, :] = turned[
                first : first + HEADS_PER_PART, :
            ]
        return carry

    lax.fori_loop(0, spans, span_terms, 0)

    for lane in REMOTE:
        meta_copy(lane).wait_recv()
    for lane in range(LANES):
        wide = jnp.broadcast_to(meta_recv[lane, 0:1, :], (128, 128))
        tall = wide.T
        for b in range(blocks):
            mask_row[lane, b] = jnp.where(wide[0:16] == b, 1.0, 0.0).astype(jnp.bfloat16)
            mask_col[lane, b] = jnp.where(tall == b, 1.0, 0.0).astype(jnp.bfloat16)

    def picked(products, ids):
        result = products[0:128]
        for b in range(1, blocks):
            result = jnp.where(ids == b, products[b * 128 : (b + 1) * 128], result)
        return result

    def score(part):
        slot_now = lax.rem(part, 3)
        for lane in REMOTE:
            span_copy(part, lane).wait_recv()
        for sub in range(HEADS_PER_PART):
            cols = pl.ds(pl.multiple_of(part * width + sub * 128, 128), 128)
            inner = slice(sub * 128, (sub + 1) * 128)
            key_rows = k_ref[:, cols]
            value_rows = v_ref[:, cols]
            bias_rows = bias_ref[
                pl.ds(pl.multiple_of((part * HEADS_PER_PART + sub) * rows, rows), rows), :
            ]
            bias_turned = jnp.concatenate([bias_rows, bias_rows], axis=0).T
            for lane in range(LANES):
                ids = meta_recv[lane, 0:1, :]
                scores = (
                    picked(rows_dot(key_rows, span_recv[part, lane, 0, :, inner]), ids) * scaling
                    + bias_turned
                )
                top = jnp.max(scores, axis=0, keepdims=True)
                lifted = jnp.exp(scores - top)
                exps[slot_now, sub, lane] = lifted
                tops[slot_now, lane, sub : sub + 1, :] = top
                target = part_recv if lane == REACH else part_send
                target[part, lane, sub : sub + 1, :] = top + jnp.log(
                    jnp.sum(lifted, axis=0, keepdims=True)
                )
                grads[slot_now, sub, lane] = picked(
                    rows_dot(value_rows, span_recv[part, lane, 1, :, inner]), ids
                )
        for lane in REMOTE:
            part_copy(part, lane).start()

    def combine(part):
        for lane in REMOTE:
            part_copy(part, lane).wait_recv()
        for lane in range(LANES):
            tile = part_recv[part, lane]
            part_pick[2 * lane] = tile
            part_pick[2 * lane + 1] = pltpu.roll(tile, rows, 1)
        for lane in range(LANES):
            s = 2 * lane
            mine = part_pick[s]
            mate = jnp.where(first_half, part_pick[partner[s]], part_pick[partner[s + 1]])
            top = jnp.maximum(mine, mate)
            total = top + jnp.log(jnp.exp(mine - top) + jnp.exp(mate - top))
            used = jnp.where(first_half, filled[s], filled[s + 1])
            total = jnp.where(used > 0, total, UNUSED)
            row = jnp.where(first_half, terms[chosen[s], part], terms[chosen[s + 1], part])
            target = total_recv if lane == REACH else total_send
            target[part, lane] = jnp.where(row_id < HEADS_PER_PART, total, row)
        for lane in REMOTE:
            total_copy(part, lane).start()

    def gradients(part):
        slot_now = lax.rem(part, 3)
        for lane in REMOTE:
            total_copy(part, lane).wait_recv()
        for sub in range(HEADS_PER_PART):
            cols = pl.ds(pl.multiple_of(part * width + sub * 128, 128), 128)
            inner = slice(sub * 128, (sub + 1) * 128)
            bias_part = jnp.zeros((128, 128), jnp.float32)
            for lane in range(LANES):
                factor = jnp.exp(
                    tops[slot_now, lane, sub : sub + 1, :] - total_recv[part, lane, sub : sub + 1, :]
                )
                row = total_recv[part, lane, HEADS_PER_PART + sub : HEADS_PER_PART + sub + 1, :]
                weights = exps[slot_now, sub, lane] * factor
                grad_scores = weights * (grads[slot_now, sub, lane] - row)
                bias_part = bias_part + grad_scores
                weights_low = weights.astype(jnp.bfloat16).reshape(8, 16, 128)
                grad_low = grad_scores.astype(jnp.bfloat16)
                grad_tall = grad_low.T
                grad_low = grad_low.reshape(8, 16, 128)
                across = slice(lane * 128, (lane + 1) * 128)
                for b in range(blocks):
                    down = slice(b * 128, (b + 1) * 128)
                    mask = mask_row[lane, b][None]
                    w_wide[down, across] = (weights_low * mask).reshape(128, 128)
                    d_wide[down, across] = (grad_low * mask).reshape(128, 128)
                    d_tall[across, down] = grad_tall * mask_col[lane, b]
            dq = (plain_dot(d_tall[...], k_ref[:, cols]) * scaling).astype(jnp.bfloat16)
            for lane in range(LANES):
                target = dq_recv if lane == REACH else dq_send
                target[part, lane, :, inner] = dq[lane * 128 : (lane + 1) * 128]
            bias_turned = bias_part.T
            bias_sum[
                pl.ds(pl.multiple_of((part * HEADS_PER_PART + sub) * rows, rows), rows), :
            ] = bias_turned[0:rows] + bias_turned[rows : 2 * rows]
            queries = span_recv[part, :, 0, :, inner].reshape(LANES * 128, 128)
            cotangents = span_recv[part, :, 1, :, inner].reshape(LANES * 128, 128)
            kg_hold[part, :, inner] = plain_dot(d_wide[...], queries) * scaling
            vg_hold[part, :, inner] = plain_dot(w_wide[...], cotangents)
        for lane in REMOTE:
            dq_copy(part, lane).start()
        hold_copy(part, 0).start()
        hold_copy(part, 1).start()

    def gather(part):
        columns = pl.ds(pl.multiple_of(part * width, width), width)
        for lane in REMOTE:
            dq_copy(part, lane).wait_recv()
        for lane in range(LANES):
            for half in range(CAP):
                dq_pick[lane * CAP + half] = dq_recv[
                    part, lane, half * rows : (half + 1) * rows, :
                ].astype(jnp.float32)
        for span in range(spans):
            both = dq_pick[place[2 * span]] + dq_pick[place[2 * span + 1]]
            qg_ref[span, :, columns] = both.astype(jnp.bfloat16)

    def step(t, carry):
        @pl.when(t + AHEAD < parts)
        def _():
            pack(t + AHEAD)
            send_spans(t + AHEAD)

        @pl.when(t < parts)
        def _():
            score(t)

        @pl.when((t >= 1) & (t < parts + 1))
        def _():
            combine(t - 1)

        @pl.when((t >= 2) & (t < parts + 2))
        def _():
            gradients(t - 2)

        @pl.when(t >= 3)
        def _():
            gather(t - 3)

        return carry

    lax.fori_loop(0, parts + 3, step, 0)

    half_rows = bias_sum.shape[0] // 2
    core_copy = pltpu.make_async_remote_copy(
        src_ref=bias_sum.at[pl.ds(pl.multiple_of((1 - dp) * half_rows, half_rows), half_rows)],
        dst_ref=core_recv,
        send_sem=core_ss,
        recv_sem=core_rs,
        device_id=(1 - dp, me),
        device_id_type=MESH,
    )
    core_copy.start()
    core_copy.wait_recv()
    mine = pl.ds(pl.multiple_of(dp * half_rows, half_rows), half_rows)
    z_send[...] = (bias_sum[mine, :] + core_recv[...]).reshape(z_send.shape)
    started = [core_copy]
    stages = ((0, at_z, z_send, z_recv), (1, at_x, x_send, x_recv), (2, at_y, y_send, y_recv))
    for axis, at, held, landed in stages:
        copies = []
        for ahead in (1, 2, 3):
            other = (at + ahead) % 4
            copies.append(
                pltpu.make_async_remote_copy(
                    src_ref=held.at[other],
                    dst_ref=landed.at[ahead - 1],
                    send_sem=ring_ss.at[axis, ahead - 1],
                    recv_sem=ring_rs.at[axis, ahead - 1],
                    device_id=ring_peers[3 * (ahead - 1) + axis],
                    device_id_type=MESH,
                )
            )
            copies[-1].start()
        for copy in copies:
            copy.wait_recv()
        total = held[at] + landed[0] + landed[1] + landed[2]
        if axis == 0:
            x_send[...] = total.reshape(x_send.shape)
        elif axis == 1:
            y_send[...] = total.reshape(y_send.shape)
        else:
            bg_ref[...] = total
        started += copies
    for copy in started:
        copy.wait_send()
    for lane in REMOTE:
        meta_copy(lane).wait_send()

    def finish(part, carry):
        for lane in REMOTE:
            span_copy(part, lane).wait_send()
            part_copy(part, lane).wait_send()
            total_copy(part, lane).wait_send()
            dq_copy(part, lane).wait_send()
        hold_copy(part, 0).wait()
        hold_copy(part, 1).wait()
        return carry

    lax.fori_loop(0, parts, finish, 0)


def per_device(queries, outputs, out_grad, keys, values, owner, slot, pos_bias):
    spans, rows, feat = queries.shape
    blocks, block_len, _ = keys.shape
    heads = pos_bias.shape[0] // rows
    head_size = feat // heads
    parts = heads // HEADS_PER_PART
    width = HEADS_PER_PART * head_size
    seq_count = lax.axis_size("seq")
    key_count = blocks * block_len
    cfg = (spans, rows, seq_count, parts, blocks, head_size ** (-0.5))
    vmem = pl.BlockSpec(memory_space=pltpu.VMEM)
    smem = pl.BlockSpec(memory_space=pltpu.SMEM)
    anywhere = pl.BlockSpec(memory_space=pl.ANY)
    f32, bf16 = jnp.float32, jnp.bfloat16
    two = CAP * rows
    bias_rows = heads * rows
    dma = pltpu.SemaphoreType.DMA
    scratch = [
        pltpu.VMEM((LANES, 8, two), f32),
        pltpu.VMEM((LANES, 8, two), f32),
        pltpu.VMEM((LANES, blocks, 16, two), bf16),
        pltpu.VMEM((LANES, blocks, two, block_len), bf16),
        pltpu.VMEM((spans, parts, 8, two), f32),
        pltpu.VMEM((parts, LANES, 2, two, width), bf16),
        pltpu.VMEM((parts, LANES, 2, two, width), bf16),
        pltpu.VMEM((parts, LANES, 8, two), f32),
        pltpu.VMEM((parts, LANES, 8, two), f32),
        pltpu.VMEM((SLOTS, 8, two), f32),
        pltpu.VMEM((parts, LANES, 8, two), f32),
        pltpu.VMEM((parts, LANES, 8, two), f32),
        pltpu.VMEM((3, LANES, 8, two), f32),
        pltpu.VMEM((3, HEADS_PER_PART, LANES, block_len, two), f32),
        pltpu.VMEM((3, HEADS_PER_PART, LANES, block_len, two), f32),
        pltpu.VMEM((key_count, LANES * two), bf16),
        pltpu.VMEM((key_count, LANES * two), bf16),
        pltpu.VMEM((LANES * two, key_count), bf16),
        pltpu.VMEM((parts, LANES, two, width), bf16),
        pltpu.VMEM((parts, LANES, two, width), bf16),
        pltpu.VMEM((SLOTS, rows, width), f32),
        pltpu.VMEM((parts, key_count, width), f32),
        pltpu.VMEM((parts, key_count, width), f32),
        pltpu.VMEM((bias_rows, block_len), f32),
        pltpu.VMEM((bias_rows // 2, block_len), f32),
        pltpu.VMEM((4, bias_rows // 8, block_len), f32),
        pltpu.VMEM((3, bias_rows // 8, block_len), f32),
        pltpu.VMEM((4, bias_rows // 32, block_len), f32),
        pltpu.VMEM((3, bias_rows // 32, block_len), f32),
        pltpu.VMEM((4, bias_rows // 128, block_len), f32),
        pltpu.VMEM((3, bias_rows // 128, block_len), f32),
        dma((LANES,)),
        dma((LANES,)),
    ]
    scratch += [dma((parts, LANES)) for _ in range(8)]
    scratch += [dma((2, parts)), dma, dma, dma((3, 3)), dma((3, 3))]
    pair_work = SLOTS * rows * key_count * feat
    call = pl.pallas_call(
        functools.partial(kernel, cfg),
        out_shape=(
            jax.ShapeDtypeStruct((spans, rows, feat), bf16),
            jax.ShapeDtypeStruct((key_count, feat), f32),
            jax.ShapeDtypeStruct((key_count, feat), f32),
            jax.ShapeDtypeStruct((bias_rows // 128, block_len), f32),
        ),
        in_specs=[smem, smem] + [vmem] * 6,
        out_specs=(vmem, anywhere, anywhere, vmem),
        scratch_shapes=scratch,
        compiler_params=pltpu.CompilerParams(
            collective_id=0, has_side_effects=True, vmem_limit_bytes=56 * 2**20
        ),
        cost_estimate=pl.CostEstimate(
            flops=10 * pair_work, bytes_accessed=20 * 2**20, transcendentals=0
        ),
    )
    query_grad, key_grad, value_grad, bias_grad = call(
        owner,
        slot,
        queries,
        outputs,
        out_grad,
        keys.reshape(key_count, feat),
        values.reshape(key_count, feat),
        pos_bias,
    )
    return (
        query_grad,
        key_grad.reshape(blocks, block_len, feat),
        value_grad.reshape(blocks, block_len, feat),
        bias_grad,
    )


def solution(mesh):
    rows = P(("dp", "seq"), None, None)
    pairs = P(("dp", "seq"), None)
    return jax.shard_map(
        per_device,
        mesh=mesh,
        in_specs=(rows, rows, rows, rows, rows, pairs, pairs, P()),
        out_specs=(rows, rows, rows, pairs),
        check_vma=False,
    )
```

```python
import functools

import jax
import jax.numpy as jnp
from jax import lax
from jax.experimental import pallas as pl
from jax.experimental.pallas import tpu as pltpu
from jax.sharding import PartitionSpec as P

REACH = 2
CAP = 2
LANES = 2 * REACH + 1
SLOTS = LANES * CAP
HEADS_PER_PART = 2
AHEAD = 2
UNUSED = 1e30
MESH = pl.DeviceIdType.MESH
REMOTE = tuple(lane for lane in range(LANES) if lane != REACH)


def rows_dot(a, b):
    return lax.dot_general(a, b, (((1,), (1,)), ((), ())), preferred_element_type=jnp.float32)


def plain_dot(a, b):
    return jnp.dot(a, b, preferred_element_type=jnp.float32)


def kernel(
    cfg,
    owner_ref,
    slot_ref,
    q_hbm,
    o_hbm,
    g_hbm,
    k_hbm,
    v_hbm,
    bias_hbm,
    qg_ref,
    kg_ref,
    vg_ref,
    bg_ref,
    q_ref,
    o_ref,
    g_ref,
    k_ref,
    v_ref,
    bias_ref,
    meta_send,
    meta_recv,
    mask_row,
    mask_col,
    terms,
    q_send,
    q_recv,
    g_send,
    g_recv,
    part_send,
    part_recv,
    part_pick,
    total_send,
    total_recv,
    tops,
    exps,
    w_wide,
    d_wide,
    d_tall,
    dq_send,
    dq_recv,
    dq_pick,
    kg_hold,
    vg_hold,
    bias_sum,
    core_recv,
    z_send,
    z_recv,
    xy_send,
    xy_recv,
    load_sem,
    meta_ss,
    meta_rs,
    q_ss,
    q_rs,
    g_ss,
    g_rs,
    part_ss,
    part_rs,
    total_ss,
    total_rs,
    dq_ss,
    dq_rs,
    hold_sem,
    core_ss,
    core_rs,
    z_ss,
    z_rs,
    xy_ss,
    xy_rs,
):
    spans, rows, seq_count, parts, blocks, scaling = cfg
    width = HEADS_PER_PART * 128
    pairs = 2 * spans
    dp = lax.axis_index("dp")
    me = lax.axis_index("seq")
    at_z, at_x, at_y = me // 16, (me // 4) % 4, me % 4

    def owner_at(lane):
        return (dp, lax.rem(me + (lane - REACH) + seq_count, seq_count))

    def asker_at(lane):
        return (dp, lax.rem(me - (lane - REACH) + seq_count, seq_count))

    def along_z(z):
        return (dp, z * 16 + at_x * 4 + at_y)

    def across(turn):
        return (dp, at_z * 16 + ((at_x + turn // 4) % 4) * 4 + (at_y + turn % 4) % 4)

    inputs = (
        (q_hbm, q_ref),
        (g_hbm, g_ref),
        (k_hbm, k_ref),
        (bias_hbm, bias_ref),
        (o_hbm, o_ref),
        (v_hbm, v_ref),
    )
    loads = [
        pltpu.make_async_copy(far, near, load_sem.at[n]) for n, (far, near) in enumerate(inputs)
    ]
    load_q, load_g, load_k, load_bias, load_o, load_v = loads
    greeted = [owner_at(lane) for lane in REMOTE] + [across(turn) for turn in range(1, 16)]
    greeted += [along_z((at_z + turn) % 4) for turn in (1, 2, 3)] + [(1 - dp, me)]
    barrier = pltpu.get_barrier_semaphore()
    for device in greeted:
        pl.semaphore_signal(barrier, inc=1, device_id=device, device_id_type=MESH)
    for load in loads:
        load.start()

    lane_of = [
        lax.rem(owner_ref[p % 2, p // 2] - me + REACH + seq_count, seq_count) for p in range(pairs)
    ]
    place = []
    for p in range(pairs):
        rank = jnp.int32(0)
        for other in range(p):
            rank = rank + jnp.where(lane_of[other] == lane_of[p], 1, 0)
        place.append(jnp.minimum(lane_of[p] * CAP + rank, SLOTS - 1))
    chosen, filled, block_id, partner = [], [], [], []
    for s in range(SLOTS):
        pick, used, block, mate = jnp.int32(0), jnp.int32(0), jnp.int32(0), jnp.int32(0)
        for p in range(pairs):
            hit = place[p] == s
            pick = jnp.where(hit, p // 2, pick)
            used = jnp.where(hit, 1, used)
            block = jnp.where(hit, slot_ref[p % 2, p // 2], block)
            mate = jnp.where(hit, place[p ^ 1], mate)
        chosen.append(pick)
        filled.append(used)
        block_id.append(block)
        partner.append((mate // 2) * 2 + (mate + s) % 2)

    lane_id = lax.broadcasted_iota(jnp.int32, (8, 128), 1)
    row_id = lax.broadcasted_iota(jnp.int32, (8, 128), 0)
    first_half = lane_id < rows

    def to_owner(held, landed, sent, got, at, lane):
        return pltpu.make_async_remote_copy(
            src_ref=held.at[at],
            dst_ref=landed.at[at],
            send_sem=sent.at[at],
            recv_sem=got.at[at],
            device_id=owner_at(lane),
            device_id_type=MESH,
        )

    def to_asker(held, landed, sent, got, at, lane):
        return pltpu.make_async_remote_copy(
            src_ref=held.at[at],
            dst_ref=landed.at[at],
            send_sem=sent.at[at],
            recv_sem=got.at[at],
            device_id=asker_at(lane),
            device_id_type=MESH,
        )

    def meta_copy(lane):
        return to_owner(meta_send, meta_recv, meta_ss, meta_rs, lane, lane)

    def q_copy(part, lane):
        return to_owner(q_send, q_recv, q_ss, q_rs, (part, lane), lane)

    def g_copy(part, lane):
        return to_owner(g_send, g_recv, g_ss, g_rs, (part, lane), lane)

    def part_copy(part, lane):
        return to_asker(part_send, part_recv, part_ss, part_rs, (part, lane), lane)

    def total_copy(part, lane):
        return to_owner(total_send, total_recv, total_ss, total_rs, (part, lane), lane)

    def dq_copy(part, lane):
        return to_asker(dq_send, dq_recv, dq_ss, dq_rs, (part, lane), lane)

    def hold_copy(part, which):
        held, out = ((kg_hold, kg_ref), (vg_hold, vg_ref))[which]
        columns = pl.ds(pl.multiple_of(part * width, width), width)
        return pltpu.make_async_copy(held.at[part], out.at[:, columns], hold_sem.at[which, part])

    def core_copy(part):
        quarter = part % 4
        return pltpu.make_async_remote_copy(
            src_ref=bias_sum.at[part],
            dst_ref=core_recv.at[quarter],
            send_sem=core_ss.at[quarter],
            recv_sem=core_rs.at[quarter],
            device_id=(1 - dp, me),
            device_id_type=MESH,
        )

    def z_copy(quarter, turn):
        return pltpu.make_async_remote_copy(
            src_ref=z_send.at[quarter],
            dst_ref=z_recv.at[turn],
            send_sem=z_ss.at[quarter],
            recv_sem=z_rs.at[turn],
            device_id=along_z(quarter),
            device_id_type=MESH,
        )

    def xy_copy(turn):
        target = ((at_x + turn // 4) % 4) * 4 + (at_y + turn % 4) % 4
        return pltpu.make_async_remote_copy(
            src_ref=xy_send.at[target],
            dst_ref=xy_recv.at[turn],
            send_sem=xy_ss.at[turn],
            recv_sem=xy_rs.at[turn],
            device_id=across(turn),
            device_id_type=MESH,
        )

    def send_rows(part, source, held, landed, copy):
        columns = pl.ds(pl.multiple_of(part * width, width), width)
        for lane in range(LANES):
            target = landed if lane == REACH else held
            for half in range(CAP):
                target[part, lane, half * rows : (half + 1) * rows, :] = source[
                    chosen[lane * CAP + half], :, columns
                ]
        for lane in REMOTE:
            copy(part, lane).start()

    def send_q(part):
        send_rows(part, q_ref, q_send, q_recv, q_copy)

    def send_g(part):
        send_rows(part, g_ref, g_send, g_recv, g_copy)

    for lane in range(LANES):
        tile = jnp.where(first_half, block_id[2 * lane], block_id[2 * lane + 1])
        target = meta_recv if lane == REACH else meta_send
        target[lane] = tile.astype(jnp.float32)
    load_q.wait()
    pl.semaphore_wait(barrier, len(greeted))
    for lane in REMOTE:
        meta_copy(lane).start()
    for part in range(AHEAD):
        send_q(part)
    load_g.wait()
    load_o.wait()

    def span_terms(span, carry):
        wide_lane = lax.broadcasted_iota(jnp.int32, (rows, 128), 1)
        gathered = jnp.zeros((rows, 128), jnp.float32)
        for head in range(parts * HEADS_PER_PART):
            cols = slice(head * 128, (head + 1) * 128)
            product = g_ref[span, :, cols].astype(jnp.float32) * o_ref[span, :, cols].astype(
                jnp.float32
            )
            gathered = jnp.where(
                wide_lane == head, jnp.sum(product, axis=1, keepdims=True), gathered
            )
        turned = jnp.concatenate([gathered, gathered], axis=0).T
        for part in range(parts):
            first = part * HEADS_PER_PART
            terms[span, part, HEADS_PER_PART : 2 * HEADS_PER_PART, :] = turned[
                first : first + HEADS_PER_PART, :
            ]
        return carry

    lax.fori_loop(0, spans, span_terms, 0)
    load_k.wait()
    load_bias.wait()
    load_v.wait()

    for lane in REMOTE:
        meta_copy(lane).wait_recv()
    for lane in range(LANES):
        wide = jnp.broadcast_to(meta_recv[lane, 0:1, :], (128, 128))
        tall = wide.T
        for b in range(blocks):
            mask_row[lane, b] = jnp.where(wide[0:16] == b, 1.0, 0.0).astype(jnp.bfloat16)
            mask_col[lane, b] = jnp.where(tall == b, 1.0, 0.0).astype(jnp.bfloat16)

    def picked(products, ids):
        result = products[0:128]
        for b in range(1, blocks):
            result = jnp.where(ids == b, products[b * 128 : (b + 1) * 128], result)
        return result

    def score(part):
        slot_now = lax.rem(part, 3)
        for lane in REMOTE:
            q_copy(part, lane).wait_recv()
        for sub in range(HEADS_PER_PART):
            cols = pl.ds(pl.multiple_of(part * width + sub * 128, 128), 128)
            inner = slice(sub * 128, (sub + 1) * 128)
            key_rows = k_ref[:, cols]
            bias_rows = bias_ref[
                pl.ds(pl.multiple_of((part * HEADS_PER_PART + sub) * rows, rows), rows), :
            ]
            bias_turned = jnp.concatenate([bias_rows, bias_rows], axis=0).T
            for lane in range(LANES):
                ids = meta_recv[lane, 0:1, :]
                scores = (
                    picked(rows_dot(key_rows, q_recv[part, lane, :, inner]), ids) * scaling
                    + bias_turned
                )
                top = jnp.max(scores, axis=0, keepdims=True)
                lifted = jnp.exp(scores - top)
                exps[slot_now, sub, lane] = lifted
                tops[slot_now, lane, sub : sub + 1, :] = top
                target = part_recv if lane == REACH else part_send
                target[part, lane, sub : sub + 1, :] = top + jnp.log(
                    jnp.sum(lifted, axis=0, keepdims=True)
                )
        for lane in REMOTE:
            part_copy(part, lane).start()

    def combine(part):
        for lane in REMOTE:
            part_copy(part, lane).wait_recv()
        for lane in range(LANES):
            tile = part_recv[part, lane]
            part_pick[2 * lane] = tile
            part_pick[2 * lane + 1] = pltpu.roll(tile, rows, 1)
        for lane in range(LANES):
            s = 2 * lane
            mine = part_pick[s]
            mate = jnp.where(first_half, part_pick[partner[s]], part_pick[partner[s + 1]])
            top = jnp.maximum(mine, mate)
            total = top + jnp.log(jnp.exp(mine - top) + jnp.exp(mate - top))
            used = jnp.where(first_half, filled[s], filled[s + 1])
            total = jnp.where(used > 0, total, UNUSED)
            row = jnp.where(first_half, terms[chosen[s], part], terms[chosen[s + 1], part])
            target = total_recv if lane == REACH else total_send
            target[part, lane] = jnp.where(row_id < HEADS_PER_PART, total, row)
        for lane in REMOTE:
            total_copy(part, lane).start()

    def gradients(part):
        slot_now = lax.rem(part, 3)
        for lane in REMOTE:
            total_copy(part, lane).wait_recv()
            g_copy(part, lane).wait_recv()
        for sub in range(HEADS_PER_PART):
            cols = pl.ds(pl.multiple_of(part * width + sub * 128, 128), 128)
            inner = slice(sub * 128, (sub + 1) * 128)
            value_rows = v_ref[:, cols]
            bias_part = jnp.zeros((128, 128), jnp.float32)
            for lane in range(LANES):
                ids = meta_recv[lane, 0:1, :]
                grad_weights = picked(rows_dot(value_rows, g_recv[part, lane, :, inner]), ids)
                factor = jnp.exp(
                    tops[slot_now, lane, sub : sub + 1, :] - total_recv[part, lane, sub : sub + 1, :]
                )
                row = total_recv[part, lane, HEADS_PER_PART + sub : HEADS_PER_PART + sub + 1, :]
                weights = exps[slot_now, sub, lane] * factor
                grad_scores = weights * (grad_weights - row)
                bias_part = bias_part + grad_scores
                weights_low = weights.astype(jnp.bfloat16).reshape(8, 16, 128)
                grad_low = grad_scores.astype(jnp.bfloat16)
                grad_tall = grad_low.T
                grad_low = grad_low.reshape(8, 16, 128)
                beside = slice(lane * 128, (lane + 1) * 128)
                for b in range(blocks):
                    down = slice(b * 128, (b + 1) * 128)
                    mask = mask_row[lane, b][None]
                    w_wide[sub, down, beside] = (weights_low * mask).reshape(128, 128)
                    d_wide[sub, down, beside] = (grad_low * mask).reshape(128, 128)
                    d_tall[beside, down] = grad_tall * mask_col[lane, b]
            dq = (plain_dot(d_tall[...], k_ref[:, cols]) * scaling).astype(jnp.bfloat16)
            for lane in range(LANES):
                target = dq_recv if lane == REACH else dq_send
                target[part, lane, :, inner] = dq[lane * 128 : (lane + 1) * 128]
            bias_turned = bias_part.T
            bias_sum[part, sub * rows : (sub + 1) * rows, :] = (
                bias_turned[0:rows] + bias_turned[rows : 2 * rows]
            )
        for lane in REMOTE:
            dq_copy(part, lane).start()

        @pl.when(part // 4 != dp)
        def _():
            core_copy(part).start()

        for sub in range(HEADS_PER_PART):
            inner = slice(sub * 128, (sub + 1) * 128)
            queries = q_recv[part, :, :, inner].reshape(LANES * 128, 128)
            cotangents = g_recv[part, :, :, inner].reshape(LANES * 128, 128)
            kg_hold[part, :, inner] = plain_dot(d_wide[sub], queries) * scaling
            vg_hold[part, :, inner] = plain_dot(w_wide[sub], cotangents)
        hold_copy(part, 0).start()
        hold_copy(part, 1).start()

    def reduce_cores(part):
        quarter = part % 4

        @pl.when(part // 4 == dp)
        def _():
            core_copy(part).wait_recv()
            z_send[quarter] = bias_sum[part] + core_recv[quarter]

            @pl.when(quarter != at_z)
            def _():
                z_copy(quarter, (at_z - quarter + 4) % 4 - 1).start()

    def gather(part):
        columns = pl.ds(pl.multiple_of(part * width, width), width)
        for lane in REMOTE:
            dq_copy(part, lane).wait_recv()
        for lane in range(LANES):
            for half in range(CAP):
                dq_pick[lane * CAP + half] = dq_recv[
                    part, lane, half * rows : (half + 1) * rows, :
                ].astype(jnp.float32)
        for span in range(spans):
            both = dq_pick[place[2 * span]] + dq_pick[place[2 * span + 1]]
            qg_ref[span, :, columns] = both.astype(jnp.bfloat16)

    def step(t, carry):
        @pl.when(t + AHEAD < parts)
        def _():
            send_q(t + AHEAD)

        @pl.when(t < parts)
        def _():
            send_g(t)
            score(t)

        @pl.when((t >= 1) & (t < parts + 1))
        def _():
            combine(t - 1)

        @pl.when(t >= 2)
        def _():
            gradients(t - 2)

        @pl.when(t >= 3)
        def _():
            reduce_cores(t - 3)
            gather(t - 3)

        return carry

    lax.fori_loop(0, parts + 2, step, 0)

    reduce_cores(parts - 1)
    for turn in range(3):
        z_copy(at_z, turn).wait_recv()
    mine = z_send[at_z] + z_recv[0] + z_recv[1] + z_recv[2]
    xy_send[...] = mine.reshape(16, 8, 128)
    for turn in range(1, 16):
        xy_copy(turn).start()
    gather(parts - 1)
    for turn in range(1, 16):
        xy_copy(turn).wait_recv()
    total = xy_send[at_x * 4 + at_y]
    for turn in range(1, 16):
        total = total + xy_recv[turn]
    bg_ref[...] = total
    for turn in range(1, 16):
        xy_copy(turn).wait_send()
    for lane in REMOTE:
        meta_copy(lane).wait_send()

    def finish(part, carry):
        for lane in REMOTE:
            q_copy(part, lane).wait_send()
            g_copy(part, lane).wait_send()
            part_copy(part, lane).wait_send()
            total_copy(part, lane).wait_send()
            dq_copy(part, lane).wait_send()

        @pl.when(part // 4 != dp)
        def _():
            core_copy(part).wait_send()

        @pl.when((part // 4 == dp) & (part % 4 != at_z))
        def _():
            z_copy(part % 4, (at_z - part % 4 + 4) % 4 - 1).wait_send()

        hold_copy(part, 0).wait()
        hold_copy(part, 1).wait()
        return carry

    lax.fori_loop(0, parts, finish, 0)


def per_device(queries, outputs, out_grad, keys, values, owner, slot, pos_bias):
    spans, rows, feat = queries.shape
    blocks, block_len, _ = keys.shape
    heads = pos_bias.shape[0] // rows
    head_size = feat // heads
    parts = heads // HEADS_PER_PART
    width = HEADS_PER_PART * head_size
    seq_count = lax.axis_size("seq")
    key_count = blocks * block_len
    cfg = (spans, rows, seq_count, parts, blocks, head_size ** (-0.5))
    vmem = pl.BlockSpec(memory_space=pltpu.VMEM)
    smem = pl.BlockSpec(memory_space=pltpu.SMEM)
    anywhere = pl.BlockSpec(memory_space=pl.ANY)
    f32, bf16 = jnp.float32, jnp.bfloat16
    two = CAP * rows
    bias_rows = heads * rows
    dma = pltpu.SemaphoreType.DMA
    near = [queries, outputs, out_grad]
    scratch = [pltpu.VMEM(array.shape, array.dtype) for array in near]
    scratch += [
        pltpu.VMEM((key_count, feat), bf16),
        pltpu.VMEM((key_count, feat), bf16),
        pltpu.VMEM(pos_bias.shape, f32),
        pltpu.VMEM((LANES, 8, two), f32),
        pltpu.VMEM((LANES, 8, two), f32),
        pltpu.VMEM((LANES, blocks, 16, two), bf16),
        pltpu.VMEM((LANES, blocks, two, block_len), bf16),
        pltpu.VMEM((spans, parts, 8, two), f32),
        pltpu.VMEM((parts, LANES, two, width), bf16),
        pltpu.VMEM((parts, LANES, two, width), bf16),
        pltpu.VMEM((parts, LANES, two, width), bf16),
        pltpu.VMEM((parts, LANES, two, width), bf16),
        pltpu.VMEM((parts, LANES, 8, two), f32),
        pltpu.VMEM((parts, LANES, 8, two), f32),
        pltpu.VMEM((SLOTS, 8, two), f32),
        pltpu.VMEM((parts, LANES, 8, two), f32),
        pltpu.VMEM((parts, LANES, 8, two), f32),
        pltpu.VMEM((3, LANES, 8, two), f32),
        pltpu.VMEM((3, HEADS_PER_PART, LANES, block_len, two), f32),
        pltpu.VMEM((HEADS_PER_PART, key_count, LANES * two), bf16),
        pltpu.VMEM((HEADS_PER_PART, key_count, LANES * two), bf16),
        pltpu.VMEM((LANES * two, key_count), bf16),
        pltpu.VMEM((parts, LANES, two, width), bf16),
        pltpu.VMEM((parts, LANES, two, width), bf16),
        pltpu.VMEM((SLOTS, rows, width), f32),
        pltpu.VMEM((parts, key_count, width), f32),
        pltpu.VMEM((parts, key_count, width), f32),
        pltpu.VMEM((parts, bias_rows // parts, block_len), f32),
        pltpu.VMEM((4, bias_rows // parts, block_len), f32),
        pltpu.VMEM((4, bias_rows // parts, block_len), f32),
        pltpu.VMEM((3, bias_rows // parts, block_len), f32),
        pltpu.VMEM((16, bias_rows // 128, block_len), f32),
        pltpu.VMEM((16, bias_rows // 128, block_len), f32),
        dma((6,)),
        dma((LANES,)),
        dma((LANES,)),
    ]
    scratch += [dma((parts, LANES)) for _ in range(10)]
    scratch += [dma((2, parts)), dma((4,)), dma((4,)), dma((4,)), dma((3,)), dma((16,)), dma((16,))]
    pair_work = SLOTS * rows * key_count * feat
    call = pl.pallas_call(
        functools.partial(kernel, cfg),
        out_shape=(
            jax.ShapeDtypeStruct((spans, rows, feat), bf16),
            jax.ShapeDtypeStruct((key_count, feat), f32),
            jax.ShapeDtypeStruct((key_count, feat), f32),
            jax.ShapeDtypeStruct((bias_rows // 128, block_len), f32),
        ),
        in_specs=[smem, smem] + [anywhere] * 6,
        out_specs=(vmem, anywhere, anywhere, vmem),
        scratch_shapes=scratch,
        compiler_params=pltpu.CompilerParams(
            collective_id=0, has_side_effects=True, vmem_limit_bytes=56 * 2**20
        ),
        cost_estimate=pl.CostEstimate(
            flops=10 * pair_work, bytes_accessed=20 * 2**20, transcendentals=0
        ),
    )
    query_grad, key_grad, value_grad, bias_grad = call(
        owner.T,
        slot.T,
        queries,
        outputs,
        out_grad,
        keys.reshape(key_count, feat),
        values.reshape(key_count, feat),
        pos_bias,
    )
    return (
        query_grad,
        key_grad.reshape(blocks, block_len, feat),
        value_grad.reshape(blocks, block_len, feat),
        bias_grad,
    )


def solution(mesh):
    rows = P(("dp", "seq"), None, None)
    pairs = P(("dp", "seq"), None)
    return jax.shard_map(
        per_device,
        mesh=mesh,
        in_specs=(rows, rows, rows, rows, rows, pairs, pairs, P()),
        out_specs=(rows, rows, rows, pairs),
        check_vma=False,
    )
```

```python
import functools

import jax
import jax.numpy as jnp
from jax import lax
from jax.experimental import pallas as pl
from jax.experimental.pallas import tpu as pltpu
from jax.sharding import PartitionSpec as P

REACH = 2
CAP = 2
LANES = 2 * REACH + 1
SLOTS = LANES * CAP
HEADS_PER_PART = 2
AHEAD = 2
FAR_AHEAD = 4
UNUSED = 1e30
MESH = pl.DeviceIdType.MESH
REMOTE = tuple(lane for lane in range(LANES) if lane != REACH)
NEAR = (REACH - 1, REACH + 1)
FAR = (0, LANES - 1)


def rows_dot(a, b):
    return lax.dot_general(a, b, (((1,), (1,)), ((), ())), preferred_element_type=jnp.float32)


def plain_dot(a, b):
    return jnp.dot(a, b, preferred_element_type=jnp.float32)


def kernel(
    cfg,
    owner_ref,
    slot_ref,
    q_hbm,
    o_hbm,
    g_hbm,
    k_hbm,
    v_hbm,
    bias_hbm,
    qg_ref,
    kg_ref,
    vg_ref,
    bg_ref,
    q_ref,
    o_ref,
    g_ref,
    k_ref,
    v_ref,
    bias_ref,
    meta_send,
    meta_recv,
    mask_row,
    mask_col,
    terms,
    q_send,
    q_recv,
    g_send,
    g_recv,
    part_send,
    part_recv,
    part_pick,
    total_send,
    total_recv,
    tops,
    exps,
    w_wide,
    d_wide,
    d_tall,
    dq_send,
    dq_recv,
    dq_pick,
    bias_sum,
    core_recv,
    z_send,
    z_recv,
    xy_send,
    xy_recv,
    load_sem,
    meta_ss,
    meta_rs,
    q_ss,
    q_rs,
    g_ss,
    g_rs,
    part_ss,
    part_rs,
    total_ss,
    total_rs,
    dq_ss,
    dq_rs,
    core_ss,
    core_rs,
    z_ss,
    z_rs,
    xy_ss,
    xy_rs,
):
    spans, rows, seq_count, parts, blocks, scaling = cfg
    width = HEADS_PER_PART * 128
    pairs = 2 * spans
    dp = lax.axis_index("dp")
    me = lax.axis_index("seq")
    at_z, at_x, at_y = me // 16, (me // 4) % 4, me % 4

    def owner_at(lane):
        return (dp, lax.rem(me + (lane - REACH) + seq_count, seq_count))

    def asker_at(lane):
        return (dp, lax.rem(me - (lane - REACH) + seq_count, seq_count))

    def along_z(z):
        return (dp, z * 16 + at_x * 4 + at_y)

    def across(turn):
        return (dp, at_z * 16 + ((at_x + turn // 4) % 4) * 4 + (at_y + turn % 4) % 4)

    inputs = (
        (q_hbm, q_ref),
        (g_hbm, g_ref),
        (k_hbm, k_ref),
        (bias_hbm, bias_ref),
        (o_hbm, o_ref),
        (v_hbm, v_ref),
    )
    loads = [
        pltpu.make_async_copy(far, near, load_sem.at[n]) for n, (far, near) in enumerate(inputs)
    ]
    load_q, load_g, load_k, load_bias, load_o, load_v = loads
    greeted = [owner_at(lane) for lane in REMOTE] + [across(turn) for turn in range(1, 16)]
    greeted += [along_z((at_z + turn) % 4) for turn in (1, 2, 3)] + [(1 - dp, me)]
    barrier = pltpu.get_barrier_semaphore()
    for device in greeted:
        pl.semaphore_signal(barrier, inc=1, device_id=device, device_id_type=MESH)
    for load in loads:
        load.start()

    lane_of = [
        lax.rem(owner_ref[p % 2, p // 2] - me + REACH + seq_count, seq_count) for p in range(pairs)
    ]
    place = []
    for p in range(pairs):
        rank = jnp.int32(0)
        for other in range(p):
            rank = rank + jnp.where(lane_of[other] == lane_of[p], 1, 0)
        place.append(jnp.minimum(lane_of[p] * CAP + rank, SLOTS - 1))
    chosen, filled, block_id, partner = [], [], [], []
    for s in range(SLOTS):
        pick, used, block, mate = jnp.int32(0), jnp.int32(0), jnp.int32(0), jnp.int32(0)
        for p in range(pairs):
            hit = place[p] == s
            pick = jnp.where(hit, p // 2, pick)
            used = jnp.where(hit, 1, used)
            block = jnp.where(hit, slot_ref[p % 2, p // 2], block)
            mate = jnp.where(hit, place[p ^ 1], mate)
        chosen.append(pick)
        filled.append(used)
        block_id.append(block)
        partner.append((mate // 2) * 2 + (mate + s) % 2)

    lane_id = lax.broadcasted_iota(jnp.int32, (8, 128), 1)
    row_id = lax.broadcasted_iota(jnp.int32, (8, 128), 0)
    first_half = lane_id < rows

    def to_owner(held, landed, sent, got, at, lane):
        return pltpu.make_async_remote_copy(
            src_ref=held.at[at],
            dst_ref=landed.at[at],
            send_sem=sent.at[at],
            recv_sem=got.at[at],
            device_id=owner_at(lane),
            device_id_type=MESH,
        )

    def to_asker(held, landed, sent, got, at, lane):
        return pltpu.make_async_remote_copy(
            src_ref=held.at[at],
            dst_ref=landed.at[at],
            send_sem=sent.at[at],
            recv_sem=got.at[at],
            device_id=asker_at(lane),
            device_id_type=MESH,
        )

    def meta_copy(lane):
        return to_owner(meta_send, meta_recv, meta_ss, meta_rs, lane, lane)

    def q_copy(part, lane):
        return to_owner(q_send, q_recv, q_ss, q_rs, (part, lane), lane)

    def g_copy(part, lane):
        return to_owner(g_send, g_recv, g_ss, g_rs, (part, lane), lane)

    def part_copy(part, lane):
        return to_asker(part_send, part_recv, part_ss, part_rs, (part, lane), lane)

    def total_copy(part, lane):
        return to_owner(total_send, total_recv, total_ss, total_rs, (part, lane), lane)

    def dq_copy(part, lane):
        return to_asker(dq_send, dq_recv, dq_ss, dq_rs, (part, lane), lane)

    def core_copy(part):
        quarter = part % 4
        return pltpu.make_async_remote_copy(
            src_ref=bias_sum.at[part],
            dst_ref=core_recv.at[quarter],
            send_sem=core_ss.at[quarter],
            recv_sem=core_rs.at[quarter],
            device_id=(1 - dp, me),
            device_id_type=MESH,
        )

    def z_copy(quarter, turn):
        return pltpu.make_async_remote_copy(
            src_ref=z_send.at[quarter],
            dst_ref=z_recv.at[turn],
            send_sem=z_ss.at[quarter],
            recv_sem=z_rs.at[turn],
            device_id=along_z(quarter),
            device_id_type=MESH,
        )

    def xy_copy(turn):
        target = ((at_x + turn // 4) % 4) * 4 + (at_y + turn % 4) % 4
        return pltpu.make_async_remote_copy(
            src_ref=xy_send.at[target],
            dst_ref=xy_recv.at[turn],
            send_sem=xy_ss.at[turn],
            recv_sem=xy_rs.at[turn],
            device_id=across(turn),
            device_id_type=MESH,
        )

    def send_rows(part, source, held, landed, copy, lanes):
        columns = pl.ds(pl.multiple_of(part * width, width), width)
        for lane in lanes:
            target = landed if lane == REACH else held
            for half in range(CAP):
                target[part, lane, half * rows : (half + 1) * rows, :] = source[
                    chosen[lane * CAP + half], :, columns
                ]
        for lane in lanes:
            if lane != REACH:
                copy(part, lane).start()

    def send_q(part, lanes):
        send_rows(part, q_ref, q_send, q_recv, q_copy, lanes)

    def send_g(part, lanes):
        send_rows(part, g_ref, g_send, g_recv, g_copy, lanes)

    for lane in range(LANES):
        tile = jnp.where(first_half, block_id[2 * lane], block_id[2 * lane + 1])
        target = meta_recv if lane == REACH else meta_send
        target[lane] = tile.astype(jnp.float32)
    load_q.wait()
    pl.semaphore_wait(barrier, len(greeted))
    for lane in REMOTE:
        meta_copy(lane).start()
    for part in range(AHEAD):
        send_q(part, FAR)
        send_q(part, NEAR + (REACH,))
    load_g.wait()

    def send_far(part, carry):
        @pl.when(part < parts)
        def _():
            send_q(part, FAR)

        send_g(part - AHEAD, FAR)
        return carry

    lax.fori_loop(AHEAD, AHEAD + FAR_AHEAD, send_far, 0)
    load_o.wait()

    def span_terms(span, carry):
        wide_lane = lax.broadcasted_iota(jnp.int32, (rows, 128), 1)
        gathered = jnp.zeros((rows, 128), jnp.float32)
        for head in range(parts * HEADS_PER_PART):
            cols = slice(head * 128, (head + 1) * 128)
            product = g_ref[span, :, cols].astype(jnp.float32) * o_ref[span, :, cols].astype(
                jnp.float32
            )
            gathered = jnp.where(
                wide_lane == head, jnp.sum(product, axis=1, keepdims=True), gathered
            )
        turned = jnp.concatenate([gathered, gathered], axis=0).T
        for part in range(parts):
            first = part * HEADS_PER_PART
            terms[span, part, HEADS_PER_PART : 2 * HEADS_PER_PART, :] = turned[
                first : first + HEADS_PER_PART, :
            ]
        return carry

    lax.fori_loop(0, spans, span_terms, 0)
    load_k.wait()
    load_bias.wait()
    load_v.wait()

    for lane in REMOTE:
        meta_copy(lane).wait_recv()
    for lane in range(LANES):
        wide = jnp.broadcast_to(meta_recv[lane, 0:1, :], (128, 128))
        tall = wide.T
        for b in range(blocks):
            mask_row[lane, b] = jnp.where(wide[0:16] == b, 1.0, 0.0).astype(jnp.bfloat16)
            mask_col[lane, b] = jnp.where(tall == b, 1.0, 0.0).astype(jnp.bfloat16)

    def picked(products, ids):
        result = products[0:128]
        for b in range(1, blocks):
            result = jnp.where(ids == b, products[b * 128 : (b + 1) * 128], result)
        return result

    def score(part):
        slot_now = lax.rem(part, 3)
        for lane in REMOTE:
            q_copy(part, lane).wait_recv()
        for sub in range(HEADS_PER_PART):
            cols = pl.ds(pl.multiple_of(part * width + sub * 128, 128), 128)
            inner = slice(sub * 128, (sub + 1) * 128)
            key_rows = k_ref[:, cols]
            bias_rows = bias_ref[
                pl.ds(pl.multiple_of((part * HEADS_PER_PART + sub) * rows, rows), rows), :
            ]
            bias_turned = jnp.concatenate([bias_rows, bias_rows], axis=0).T
            for lane in range(LANES):
                ids = meta_recv[lane, 0:1, :]
                scores = (
                    picked(rows_dot(key_rows, q_recv[part, lane, :, inner]), ids) * scaling
                    + bias_turned
                )
                top = jnp.max(scores, axis=0, keepdims=True)
                lifted = jnp.exp(scores - top)
                exps[slot_now, sub, lane] = lifted
                tops[slot_now, lane, sub : sub + 1, :] = top
                target = part_recv if lane == REACH else part_send
                target[part, lane, sub : sub + 1, :] = top + jnp.log(
                    jnp.sum(lifted, axis=0, keepdims=True)
                )
        for lane in REMOTE:
            part_copy(part, lane).start()

    def combine(part):
        for lane in REMOTE:
            part_copy(part, lane).wait_recv()
        for lane in range(LANES):
            tile = part_recv[part, lane]
            part_pick[2 * lane] = tile
            part_pick[2 * lane + 1] = pltpu.roll(tile, rows, 1)
        for lane in range(LANES):
            s = 2 * lane
            mine = part_pick[s]
            mate = jnp.where(first_half, part_pick[partner[s]], part_pick[partner[s + 1]])
            top = jnp.maximum(mine, mate)
            total = top + jnp.log(jnp.exp(mine - top) + jnp.exp(mate - top))
            used = jnp.where(first_half, filled[s], filled[s + 1])
            total = jnp.where(used > 0, total, UNUSED)
            row = jnp.where(first_half, terms[chosen[s], part], terms[chosen[s + 1], part])
            target = total_recv if lane == REACH else total_send
            target[part, lane] = jnp.where(row_id < HEADS_PER_PART, total, row)
        for lane in REMOTE:
            total_copy(part, lane).start()

    def gradients(part):
        slot_now = lax.rem(part, 3)
        for lane in REMOTE:
            total_copy(part, lane).wait_recv()
            g_copy(part, lane).wait_recv()
        for sub in range(HEADS_PER_PART):
            cols = pl.ds(pl.multiple_of(part * width + sub * 128, 128), 128)
            inner = slice(sub * 128, (sub + 1) * 128)
            value_rows = v_ref[:, cols]
            bias_part = jnp.zeros((128, 128), jnp.float32)
            for lane in range(LANES):
                ids = meta_recv[lane, 0:1, :]
                grad_weights = picked(rows_dot(value_rows, g_recv[part, lane, :, inner]), ids)
                factor = jnp.exp(
                    tops[slot_now, lane, sub : sub + 1, :] - total_recv[part, lane, sub : sub + 1, :]
                )
                row = total_recv[part, lane, HEADS_PER_PART + sub : HEADS_PER_PART + sub + 1, :]
                weights = exps[slot_now, sub, lane] * factor
                grad_scores = weights * (grad_weights - row)
                bias_part = bias_part + grad_scores
                weights_low = weights.astype(jnp.bfloat16).reshape(8, 16, 128)
                grad_low = grad_scores.astype(jnp.bfloat16)
                grad_tall = grad_low.T
                grad_low = grad_low.reshape(8, 16, 128)
                beside = slice(lane * 128, (lane + 1) * 128)
                for b in range(blocks):
                    down = slice(b * 128, (b + 1) * 128)
                    mask = mask_row[lane, b][None]
                    w_wide[sub, down, beside] = (weights_low * mask).reshape(128, 128)
                    d_wide[sub, down, beside] = (grad_low * mask).reshape(128, 128)
                    d_tall[beside, down] = grad_tall * mask_col[lane, b]
            dq = (plain_dot(d_tall[...], k_ref[:, cols]) * scaling).astype(jnp.bfloat16)
            for lane in range(LANES):
                target = dq_recv if lane == REACH else dq_send
                target[part, lane, :, inner] = dq[lane * 128 : (lane + 1) * 128]
            bias_turned = bias_part.T
            bias_sum[part, sub * rows : (sub + 1) * rows, :] = (
                bias_turned[0:rows] + bias_turned[rows : 2 * rows]
            )
        for lane in REMOTE:
            dq_copy(part, lane).start()

        @pl.when(part // 4 != dp)
        def _():
            core_copy(part).start()

        for sub in range(HEADS_PER_PART):
            inner = slice(sub * 128, (sub + 1) * 128)
            queries = q_recv[part, :, :, inner].reshape(LANES * 128, 128)
            cotangents = g_recv[part, :, :, inner].reshape(LANES * 128, 128)
            cols = pl.ds(pl.multiple_of(part * width + sub * 128, 128), 128)
            kg_ref[:, cols] = plain_dot(d_wide[sub], queries) * scaling
            vg_ref[:, cols] = plain_dot(w_wide[sub], cotangents)

    def reduce_cores(part):
        quarter = part % 4

        @pl.when(part // 4 == dp)
        def _():
            core_copy(part).wait_recv()
            z_send[quarter] = bias_sum[part] + core_recv[quarter]

            @pl.when(quarter != at_z)
            def _():
                z_copy(quarter, (at_z - quarter + 4) % 4 - 1).start()

    def gather(part):
        columns = pl.ds(pl.multiple_of(part * width, width), width)
        for lane in REMOTE:
            dq_copy(part, lane).wait_recv()
        for lane in range(LANES):
            for half in range(CAP):
                dq_pick[lane * CAP + half] = dq_recv[
                    part, lane, half * rows : (half + 1) * rows, :
                ].astype(jnp.float32)
        for span in range(spans):
            both = dq_pick[place[2 * span]] + dq_pick[place[2 * span + 1]]
            qg_ref[span, :, columns] = both.astype(jnp.bfloat16)

    def step(t, carry):
        @pl.when(t + FAR_AHEAD < parts)
        def _():
            send_far(t + FAR_AHEAD + AHEAD, 0)

        @pl.when(t + AHEAD < parts)
        def _():
            send_q(t + AHEAD, NEAR + (REACH,))

        @pl.when(t < parts)
        def _():
            send_g(t, NEAR + (REACH,))
            score(t)

        @pl.when((t >= 1) & (t < parts + 1))
        def _():
            combine(t - 1)

        @pl.when(t >= 2)
        def _():
            gradients(t - 2)

        @pl.when(t >= 3)
        def _():
            reduce_cores(t - 3)
            gather(t - 3)

        return carry

    lax.fori_loop(0, parts + 2, step, 0)

    reduce_cores(parts - 1)
    for turn in range(3):
        z_copy(at_z, turn).wait_recv()
    mine = z_send[at_z] + z_recv[0] + z_recv[1] + z_recv[2]
    xy_send[...] = mine.reshape(16, 8, 128)
    for turn in range(1, 16):
        xy_copy(turn).start()
    gather(parts - 1)
    for turn in range(1, 16):
        xy_copy(turn).wait_recv()
    total = xy_send[at_x * 4 + at_y]
    for turn in range(1, 16):
        total = total + xy_recv[turn]
    bg_ref[...] = total
    for turn in range(1, 16):
        xy_copy(turn).wait_send()
    for lane in REMOTE:
        meta_copy(lane).wait_send()

    def finish(part, carry):
        for lane in REMOTE:
            q_copy(part, lane).wait_send()
            g_copy(part, lane).wait_send()
            part_copy(part, lane).wait_send()
            total_copy(part, lane).wait_send()
            dq_copy(part, lane).wait_send()

        @pl.when(part // 4 != dp)
        def _():
            core_copy(part).wait_send()

        @pl.when((part // 4 == dp) & (part % 4 != at_z))
        def _():
            z_copy(part % 4, (at_z - part % 4 + 4) % 4 - 1).wait_send()

        return carry

    lax.fori_loop(0, parts, finish, 0)


def store(*refs):
    sem = refs[8]
    copies = [pltpu.make_async_copy(refs[n], refs[4 + n], sem.at[n]) for n in range(4)]
    for copy in copies:
        copy.start()
    for copy in copies:
        copy.wait()


def per_device(queries, outputs, out_grad, keys, values, owner, slot, pos_bias):
    spans, rows, feat = queries.shape
    blocks, block_len, _ = keys.shape
    heads = pos_bias.shape[0] // rows
    head_size = feat // heads
    parts = heads // HEADS_PER_PART
    width = HEADS_PER_PART * head_size
    seq_count = lax.axis_size("seq")
    key_count = blocks * block_len
    cfg = (spans, rows, seq_count, parts, blocks, head_size ** (-0.5))
    vmem = pl.BlockSpec(memory_space=pltpu.VMEM)
    smem = pl.BlockSpec(memory_space=pltpu.SMEM)
    anywhere = pl.BlockSpec(memory_space=pl.ANY)
    f32, bf16 = jnp.float32, jnp.bfloat16
    two = CAP * rows
    bias_rows = heads * rows
    dma = pltpu.SemaphoreType.DMA
    near = [queries, outputs, out_grad]
    scratch = [pltpu.VMEM(array.shape, array.dtype) for array in near]
    scratch += [
        pltpu.VMEM((key_count, feat), bf16),
        pltpu.VMEM((key_count, feat), bf16),
        pltpu.VMEM(pos_bias.shape, f32),
        pltpu.VMEM((LANES, 8, two), f32),
        pltpu.VMEM((LANES, 8, two), f32),
        pltpu.VMEM((LANES, blocks, 16, two), bf16),
        pltpu.VMEM((LANES, blocks, two, block_len), bf16),
        pltpu.VMEM((spans, parts, 8, two), f32),
        pltpu.VMEM((parts, LANES, two, width), bf16),
        pltpu.VMEM((parts, LANES, two, width), bf16),
        pltpu.VMEM((parts, LANES, two, width), bf16),
        pltpu.VMEM((parts, LANES, two, width), bf16),
        pltpu.VMEM((parts, LANES, 8, two), f32),
        pltpu.VMEM((parts, LANES, 8, two), f32),
        pltpu.VMEM((SLOTS, 8, two), f32),
        pltpu.VMEM((parts, LANES, 8, two), f32),
        pltpu.VMEM((parts, LANES, 8, two), f32),
        pltpu.VMEM((3, LANES, 8, two), f32),
        pltpu.VMEM((3, HEADS_PER_PART, LANES, block_len, two), f32),
        pltpu.VMEM((HEADS_PER_PART, key_count, LANES * two), bf16),
        pltpu.VMEM((HEADS_PER_PART, key_count, LANES * two), bf16),
        pltpu.VMEM((LANES * two, key_count), bf16),
        pltpu.VMEM((parts, LANES, two, width), bf16),
        pltpu.VMEM((parts, LANES, two, width), bf16),
        pltpu.VMEM((SLOTS, rows, width), f32),
        pltpu.VMEM((parts, bias_rows // parts, block_len), f32),
        pltpu.VMEM((4, bias_rows // parts, block_len), f32),
        pltpu.VMEM((4, bias_rows // parts, block_len), f32),
        pltpu.VMEM((3, bias_rows // parts, block_len), f32),
        pltpu.VMEM((16, bias_rows // 128, block_len), f32),
        pltpu.VMEM((16, bias_rows // 128, block_len), f32),
        dma((6,)),
        dma((LANES,)),
        dma((LANES,)),
    ]
    scratch += [dma((parts, LANES)) for _ in range(10)]
    scratch += [dma((4,)), dma((4,)), dma((4,)), dma((3,)), dma((16,)), dma((16,))]
    pair_work = SLOTS * rows * key_count * feat
    call = pl.pallas_call(
        functools.partial(kernel, cfg),
        out_shape=(
            pltpu.VMEM((spans, rows, feat), bf16),
            pltpu.VMEM((key_count, feat), f32),
            pltpu.VMEM((key_count, feat), f32),
            pltpu.VMEM((bias_rows // 128, block_len), f32),
        ),
        in_specs=[smem, smem] + [anywhere] * 6,
        out_specs=(vmem, vmem, vmem, vmem),
        scratch_shapes=scratch,
        compiler_params=pltpu.CompilerParams(
            collective_id=0, has_side_effects=True, vmem_limit_bytes=46 * 2**20
        ),
        cost_estimate=pl.CostEstimate(
            flops=10 * pair_work, bytes_accessed=20 * 2**20, transcendentals=0
        ),
    )
    results = call(
        owner.T,
        slot.T,
        queries,
        outputs,
        out_grad,
        keys.reshape(key_count, feat),
        values.reshape(key_count, feat),
        pos_bias,
    )
    query_grad, key_grad, value_grad, bias_grad = pl.pallas_call(
        store,
        out_shape=tuple(jax.ShapeDtypeStruct(r.shape, r.dtype) for r in results),
        in_specs=[vmem] * 4,
        out_specs=(anywhere,) * 4,
        scratch_shapes=[dma((4,))],
        compiler_params=pltpu.CompilerParams(vmem_limit_bytes=2**20),
    )(*results)
    return (
        query_grad,
        key_grad.reshape(blocks, block_len, feat),
        value_grad.reshape(blocks, block_len, feat),
        bias_grad,
    )


def solution(mesh):
    rows = P(("dp", "seq"), None, None)
    pairs = P(("dp", "seq"), None)
    return jax.shard_map(
        per_device,
        mesh=mesh,
        in_specs=(rows, rows, rows, rows, rows, pairs, pairs, P()),
        out_specs=(rows, rows, rows, pairs),
        check_vma=False,
    )
```

```python
import functools

import jax
import jax.numpy as jnp
from jax import lax
from jax.experimental import pallas as pl
from jax.experimental.pallas import tpu as pltpu
from jax.sharding import PartitionSpec as P

REACH = 2
CAP = 2
LANES = 2 * REACH + 1
SLOTS = LANES * CAP
HEADS_PER_PART = 2
AHEAD = 2
FAR_AHEAD = 4
HELD = 1
UNUSED = 1e30
MESH = pl.DeviceIdType.MESH
REMOTE = tuple(lane for lane in range(LANES) if lane != REACH)
NEAR = (REACH - 1, REACH + 1)
FAR = (0, LANES - 1)


def rows_dot(a, b):
    return lax.dot_general(a, b, (((1,), (1,)), ((), ())), preferred_element_type=jnp.float32)


def plain_dot(a, b):
    return jnp.dot(a, b, preferred_element_type=jnp.float32)


def kernel(
    cfg,
    owner_ref,
    slot_ref,
    q_hbm,
    o_hbm,
    g_hbm,
    k_hbm,
    v_hbm,
    bias_hbm,
    qg_ref,
    kg_ref,
    vg_ref,
    bg_ref,
    q_ref,
    o_ref,
    g_ref,
    k_ref,
    v_ref,
    bias_ref,
    meta_send,
    meta_recv,
    mask_row,
    mask_col,
    terms,
    q_send,
    q_recv,
    g_send,
    g_recv,
    part_send,
    part_recv,
    part_pick,
    total_send,
    total_recv,
    tops,
    exps,
    w_wide,
    d_wide,
    d_tall,
    dq_send,
    dq_recv,
    dq_pick,
    bias_sum,
    core_recv,
    z_send,
    z_recv,
    xy_send,
    xy_recv,
    load_sem,
    meta_ss,
    meta_rs,
    q_ss,
    q_rs,
    g_ss,
    g_rs,
    part_ss,
    part_rs,
    total_ss,
    total_rs,
    dq_ss,
    dq_rs,
    core_ss,
    core_rs,
    z_ss,
    z_rs,
    xy_ss,
    xy_rs,
):
    spans, rows, seq_count, parts, blocks, scaling = cfg
    width = HEADS_PER_PART * 128
    pairs = 2 * spans
    dp = lax.axis_index("dp")
    me = lax.axis_index("seq")
    at_z, at_x, at_y = me // 16, (me // 4) % 4, me % 4

    def owner_at(lane):
        return (dp, lax.rem(me + (lane - REACH) + seq_count, seq_count))

    def asker_at(lane):
        return (dp, lax.rem(me - (lane - REACH) + seq_count, seq_count))

    def along_z(z):
        return (dp, z * 16 + at_x * 4 + at_y)

    def across(turn):
        return (dp, at_z * 16 + ((at_x + turn // 4) % 4) * 4 + (at_y + turn % 4) % 4)

    inputs = (
        (q_hbm, q_ref),
        (g_hbm, g_ref),
        (k_hbm, k_ref),
        (bias_hbm, bias_ref),
        (o_hbm, o_ref),
        (v_hbm, v_ref),
    )
    loads = [
        pltpu.make_async_copy(far, near, load_sem.at[n]) for n, (far, near) in enumerate(inputs)
    ]
    load_q, load_g, load_k, load_bias, load_o, load_v = loads
    greeted = [owner_at(lane) for lane in REMOTE] + [across(turn) for turn in range(1, 16)]
    greeted += [along_z((at_z + turn) % 4) for turn in (1, 2, 3)] + [(1 - dp, me)]
    barrier = pltpu.get_barrier_semaphore()
    for device in greeted:
        pl.semaphore_signal(barrier, inc=1, device_id=device, device_id_type=MESH)
    for load in loads:
        load.start()

    lane_of = [
        lax.rem(owner_ref[p % 2, p // 2] - me + REACH + seq_count, seq_count) for p in range(pairs)
    ]
    place = []
    for p in range(pairs):
        rank = jnp.int32(0)
        for other in range(p):
            rank = rank + jnp.where(lane_of[other] == lane_of[p], 1, 0)
        place.append(jnp.minimum(lane_of[p] * CAP + rank, SLOTS - 1))
    chosen, filled, block_id, partner = [], [], [], []
    for s in range(SLOTS):
        pick, used, block, mate = jnp.int32(0), jnp.int32(0), jnp.int32(0), jnp.int32(0)
        for p in range(pairs):
            hit = place[p] == s
            pick = jnp.where(hit, p // 2, pick)
            used = jnp.where(hit, 1, used)
            block = jnp.where(hit, slot_ref[p % 2, p // 2], block)
            mate = jnp.where(hit, place[p ^ 1], mate)
        chosen.append(pick)
        filled.append(used)
        block_id.append(block)
        partner.append((mate // 2) * 2 + (mate + s) % 2)

    lane_id = lax.broadcasted_iota(jnp.int32, (8, 128), 1)
    row_id = lax.broadcasted_iota(jnp.int32, (8, 128), 0)
    first_half = lane_id < rows

    def to_owner(held, landed, sent, got, at, lane):
        return pltpu.make_async_remote_copy(
            src_ref=held.at[at],
            dst_ref=landed.at[at],
            send_sem=sent.at[at],
            recv_sem=got.at[at],
            device_id=owner_at(lane),
            device_id_type=MESH,
        )

    def to_asker(held, landed, sent, got, at, lane):
        return pltpu.make_async_remote_copy(
            src_ref=held.at[at],
            dst_ref=landed.at[at],
            send_sem=sent.at[at],
            recv_sem=got.at[at],
            device_id=asker_at(lane),
            device_id_type=MESH,
        )

    def meta_copy(lane):
        return to_owner(meta_send, meta_recv, meta_ss, meta_rs, lane, lane)

    def q_copy(part, lane):
        return to_owner(q_send, q_recv, q_ss, q_rs, (part, lane), lane)

    def g_copy(part, lane):
        return to_owner(g_send, g_recv, g_ss, g_rs, (part, lane), lane)

    def part_copy(part, lane):
        return to_asker(part_send, part_recv, part_ss, part_rs, (part, lane), lane)

    def total_copy(part, lane):
        return to_owner(total_send, total_recv, total_ss, total_rs, (part, lane), lane)

    def dq_copy(part, lane):
        return to_asker(dq_send, dq_recv, dq_ss, dq_rs, (part, lane), lane)

    def core_copy(part):
        quarter = part % 4
        return pltpu.make_async_remote_copy(
            src_ref=bias_sum.at[part],
            dst_ref=core_recv.at[quarter],
            send_sem=core_ss.at[quarter],
            recv_sem=core_rs.at[quarter],
            device_id=(1 - dp, me),
            device_id_type=MESH,
        )

    def z_copy(quarter, turn):
        return pltpu.make_async_remote_copy(
            src_ref=z_send.at[quarter],
            dst_ref=z_recv.at[turn],
            send_sem=z_ss.at[quarter],
            recv_sem=z_rs.at[turn],
            device_id=along_z(quarter),
            device_id_type=MESH,
        )

    def xy_copy(turn):
        target = ((at_x + turn // 4) % 4) * 4 + (at_y + turn % 4) % 4
        return pltpu.make_async_remote_copy(
            src_ref=xy_send.at[target],
            dst_ref=xy_recv.at[turn],
            send_sem=xy_ss.at[turn],
            recv_sem=xy_rs.at[turn],
            device_id=across(turn),
            device_id_type=MESH,
        )

    def pack(part, source, held, landed, lanes):
        columns = pl.ds(pl.multiple_of(part * width, width), width)
        for lane in lanes:
            target = landed if lane == REACH else held
            for half in range(CAP):
                target[part, lane, half * rows : (half + 1) * rows, :] = source[
                    chosen[lane * CAP + half], :, columns
                ]

    def start(part, copy, lanes):
        for lane in lanes:
            if lane != REACH:
                copy(part, lane).start()

    def send_q(part, lanes):
        pack(part, q_ref, q_send, q_recv, lanes)
        start(part, q_copy, lanes)

    def send_g(part, lanes):
        pack(part, g_ref, g_send, g_recv, lanes)
        start(part, g_copy, lanes)

    for lane in range(LANES):
        tile = jnp.where(first_half, block_id[2 * lane], block_id[2 * lane + 1])
        target = meta_recv if lane == REACH else meta_send
        target[lane] = tile.astype(jnp.float32)
    part_pick[...] = jnp.zeros(part_pick.shape, jnp.float32)
    load_q.wait()
    for part in range(AHEAD):
        pack(part, q_ref, q_send, q_recv, range(LANES))
    pl.semaphore_wait(barrier, len(greeted))
    for lane in REMOTE:
        meta_copy(lane).start()
    for part in range(AHEAD):
        start(part, q_copy, FAR + NEAR)
    load_g.wait()

    def send_far(part, carry):
        @pl.when(part < parts)
        def _():
            send_q(part, FAR)

        send_g(part - AHEAD, FAR)
        return carry

    lax.fori_loop(AHEAD, AHEAD + FAR_AHEAD, send_far, 0)
    load_o.wait()

    def span_terms(span, carry):
        wide_lane = lax.broadcasted_iota(jnp.int32, (rows, 128), 1)
        gathered = jnp.zeros((rows, 128), jnp.float32)
        for head in range(parts * HEADS_PER_PART):
            cols = slice(head * 128, (head + 1) * 128)
            product = g_ref[span, :, cols].astype(jnp.float32) * o_ref[span, :, cols].astype(
                jnp.float32
            )
            gathered = jnp.where(
                wide_lane == head, jnp.sum(product, axis=1, keepdims=True), gathered
            )
        turned = jnp.concatenate([gathered, gathered], axis=0).T
        for part in range(parts):
            first = part * HEADS_PER_PART
            terms[span, part, HEADS_PER_PART : 2 * HEADS_PER_PART, :] = turned[
                first : first + HEADS_PER_PART, :
            ]
        return carry

    lax.fori_loop(0, spans, span_terms, 0)
    load_k.wait()
    load_bias.wait()
    load_v.wait()

    for lane in REMOTE:
        meta_copy(lane).wait_recv()
    for lane in range(LANES):
        wide = jnp.broadcast_to(meta_recv[lane, 0:1, :], (128, 128))
        tall = wide.T
        for b in range(blocks):
            mask_row[lane, b] = jnp.where(wide[0:16] == b, 1.0, 0.0).astype(jnp.bfloat16)
            mask_col[lane, b] = jnp.where(tall == b, 1.0, 0.0).astype(jnp.bfloat16)

    def picked(products, ids):
        result = products[0:128]
        for b in range(1, blocks):
            result = jnp.where(ids == b, products[b * 128 : (b + 1) * 128], result)
        return result

    def score(part):
        slot_now = lax.rem(part, 3)
        for lane in REMOTE:
            q_copy(part, lane).wait_recv()
        for sub in range(HEADS_PER_PART):
            cols = pl.ds(pl.multiple_of(part * width + sub * 128, 128), 128)
            inner = slice(sub * 128, (sub + 1) * 128)
            key_rows = k_ref[:, cols]
            bias_rows = bias_ref[
                pl.ds(pl.multiple_of((part * HEADS_PER_PART + sub) * rows, rows), rows), :
            ]
            bias_turned = jnp.concatenate([bias_rows, bias_rows], axis=0).T
            for lane in range(LANES):
                ids = meta_recv[lane, 0:1, :]
                scores = (
                    picked(rows_dot(key_rows, q_recv[part, lane, :, inner]), ids) * scaling
                    + bias_turned
                )
                top = jnp.max(scores, axis=0, keepdims=True)
                lifted = jnp.exp(scores - top)
                exps[slot_now, sub, lane] = lifted
                tops[slot_now, lane, sub : sub + 1, :] = top
                target = part_recv if lane == REACH else part_send
                target[part, lane, sub : sub + 1, :] = top + jnp.log(
                    jnp.sum(lifted, axis=0, keepdims=True)
                )
        for lane in REMOTE:
            part_copy(part, lane).start()

    def combine(part):
        for lane in REMOTE:
            part_copy(part, lane).wait_recv()
        for lane in range(LANES):
            part_pick[2 * lane, 0:HEADS_PER_PART, :] = part_recv[part, lane]
            part_pick[2 * lane + 1] = pltpu.roll(part_pick[2 * lane], rows, 1)
        for lane in range(LANES):
            s = 2 * lane
            mine = part_pick[s]
            mate = jnp.where(first_half, part_pick[partner[s]], part_pick[partner[s + 1]])
            top = jnp.maximum(mine, mate)
            total = top + jnp.log(jnp.exp(mine - top) + jnp.exp(mate - top))
            used = jnp.where(first_half, filled[s], filled[s + 1])
            total = jnp.where(used > 0, total, UNUSED)
            row = jnp.where(first_half, terms[chosen[s], part], terms[chosen[s + 1], part])
            target = total_recv if lane == REACH else total_send
            target[part, lane] = jnp.where(row_id < HEADS_PER_PART, total, row)[
                0 : 2 * HEADS_PER_PART
            ]
        for lane in REMOTE:
            total_copy(part, lane).start()

    def send_dq(part, carry):
        for lane in REMOTE:
            dq_copy(part, lane).start()
        return carry

    def gradients(part):
        slot_now = lax.rem(part, 3)
        for lane in REMOTE:
            total_copy(part, lane).wait_recv()
            g_copy(part, lane).wait_recv()

        @pl.when(part >= HELD + 1)
        def _():
            send_dq(part - HELD - 1, 0)

        @pl.when(part == parts - 1)
        def _():
            lax.fori_loop(parts - 1 - HELD, parts - 1, send_dq, 0)

        for sub in range(HEADS_PER_PART):
            cols = pl.ds(pl.multiple_of(part * width + sub * 128, 128), 128)
            inner = slice(sub * 128, (sub + 1) * 128)
            value_rows = v_ref[:, cols]
            bias_part = jnp.zeros((128, 128), jnp.float32)
            for lane in range(LANES):
                ids = meta_recv[lane, 0:1, :]
                grad_weights = picked(rows_dot(value_rows, g_recv[part, lane, :, inner]), ids)
                factor = jnp.exp(
                    tops[slot_now, lane, sub : sub + 1, :] - total_recv[part, lane, sub : sub + 1, :]
                )
                row = total_recv[part, lane, HEADS_PER_PART + sub : HEADS_PER_PART + sub + 1, :]
                weights = exps[slot_now, sub, lane] * factor
                grad_scores = weights * (grad_weights - row)
                bias_part = bias_part + grad_scores
                weights_low = weights.astype(jnp.bfloat16).reshape(8, 16, 128)
                grad_low = grad_scores.astype(jnp.bfloat16)
                grad_tall = grad_low.T
                grad_low = grad_low.reshape(8, 16, 128)
                beside = slice(lane * 128, (lane + 1) * 128)
                for b in range(blocks):
                    down = slice(b * 128, (b + 1) * 128)
                    mask = mask_row[lane, b][None]
                    w_wide[sub, down, beside] = (weights_low * mask).reshape(128, 128)
                    d_wide[sub, down, beside] = (grad_low * mask).reshape(128, 128)
                    d_tall[beside, down] = grad_tall * mask_col[lane, b]
            dq = (plain_dot(d_tall[...], k_ref[:, cols]) * scaling).astype(jnp.bfloat16)
            for lane in range(LANES):
                target = dq_recv if lane == REACH else dq_send
                target[part, lane, :, inner] = dq[lane * 128 : (lane + 1) * 128]
            bias_turned = bias_part.T
            bias_sum[part, sub * rows : (sub + 1) * rows, :] = (
                bias_turned[0:rows] + bias_turned[rows : 2 * rows]
            )
        @pl.when(part == parts - 1)
        def _():
            send_dq(part, 0)

        @pl.when(part // 4 != dp)
        def _():
            core_copy(part).start()

        for sub in range(HEADS_PER_PART):
            inner = slice(sub * 128, (sub + 1) * 128)
            queries = q_recv[part, :, :, inner].reshape(LANES * 128, 128)
            cotangents = g_recv[part, :, :, inner].reshape(LANES * 128, 128)
            cols = pl.ds(pl.multiple_of(part * width + sub * 128, 128), 128)
            kg_ref[:, cols] = plain_dot(d_wide[sub], queries) * scaling
            vg_ref[:, cols] = plain_dot(w_wide[sub], cotangents)

    def reduce_cores(part):
        quarter = part % 4

        @pl.when(part // 4 == dp)
        def _():
            core_copy(part).wait_recv()
            z_send[quarter] = bias_sum[part] + core_recv[quarter]

            @pl.when(quarter != at_z)
            def _():
                z_copy(quarter, (at_z - quarter + 4) % 4 - 1).start()

    def gather(part, carry):
        columns = pl.ds(pl.multiple_of(part * width, width), width)
        for lane in REMOTE:
            dq_copy(part, lane).wait_recv()
        for lane in range(LANES):
            for half in range(CAP):
                dq_pick[lane * CAP + half] = dq_recv[
                    part, lane, half * rows : (half + 1) * rows, :
                ].astype(jnp.float32)
        for span in range(spans):
            both = dq_pick[place[2 * span]] + dq_pick[place[2 * span + 1]]
            qg_ref[span, :, columns] = both.astype(jnp.bfloat16)
        return carry

    def step(t, carry):
        @pl.when(t + FAR_AHEAD < parts)
        def _():
            send_far(t + FAR_AHEAD + AHEAD, 0)

        @pl.when(t + AHEAD < parts)
        def _():
            send_q(t + AHEAD, NEAR + (REACH,))

        @pl.when(t < parts)
        def _():
            send_g(t, NEAR + (REACH,))
            score(t)

        @pl.when((t >= 1) & (t < parts + 1))
        def _():
            combine(t - 1)

        @pl.when(t >= 2)
        def _():
            gradients(t - 2)

        @pl.when(t >= 3)
        def _():
            reduce_cores(t - 3)

        @pl.when(t >= HELD + 4)
        def _():
            gather(t - HELD - 4, 0)

        return carry

    lax.fori_loop(0, parts + 2, step, 0)

    reduce_cores(parts - 1)
    for turn in range(3):
        z_copy(at_z, turn).wait_recv()
    mine = z_send[at_z] + z_recv[0] + z_recv[1] + z_recv[2]
    xy_send[...] = mine.reshape(16, 8, 128)
    for turn in range(1, 16):
        xy_copy(turn).start()
    lax.fori_loop(parts - HELD - 2, parts, gather, 0)
    for turn in range(1, 16):
        xy_copy(turn).wait_recv()
    total = xy_send[at_x * 4 + at_y]
    for turn in range(1, 16):
        total = total + xy_recv[turn]
    bg_ref[...] = total
    for turn in range(1, 16):
        xy_copy(turn).wait_send()
    for lane in REMOTE:
        meta_copy(lane).wait_send()

    def finish(part, carry):
        for lane in REMOTE:
            q_copy(part, lane).wait_send()
            g_copy(part, lane).wait_send()
            part_copy(part, lane).wait_send()
            total_copy(part, lane).wait_send()
            dq_copy(part, lane).wait_send()

        @pl.when(part // 4 != dp)
        def _():
            core_copy(part).wait_send()

        @pl.when((part // 4 == dp) & (part % 4 != at_z))
        def _():
            z_copy(part % 4, (at_z - part % 4 + 4) % 4 - 1).wait_send()

        return carry

    lax.fori_loop(0, parts, finish, 0)


def store(*refs):
    sem = refs[8]
    copies = [pltpu.make_async_copy(refs[n], refs[4 + n], sem.at[n]) for n in range(4)]
    for copy in copies:
        copy.start()
    for copy in copies:
        copy.wait()


def per_device(queries, outputs, out_grad, keys, values, owner, slot, pos_bias):
    spans, rows, feat = queries.shape
    blocks, block_len, _ = keys.shape
    heads = pos_bias.shape[0] // rows
    head_size = feat // heads
    parts = heads // HEADS_PER_PART
    width = HEADS_PER_PART * head_size
    seq_count = lax.axis_size("seq")
    key_count = blocks * block_len
    cfg = (spans, rows, seq_count, parts, blocks, head_size ** (-0.5))
    vmem = pl.BlockSpec(memory_space=pltpu.VMEM)
    smem = pl.BlockSpec(memory_space=pltpu.SMEM)
    anywhere = pl.BlockSpec(memory_space=pl.ANY)
    f32, bf16 = jnp.float32, jnp.bfloat16
    two = CAP * rows
    bias_rows = heads * rows
    dma = pltpu.SemaphoreType.DMA
    near = [queries, outputs, out_grad]
    scratch = [pltpu.VMEM(array.shape, array.dtype) for array in near]
    scratch += [
        pltpu.VMEM((key_count, feat), bf16),
        pltpu.VMEM((key_count, feat), bf16),
        pltpu.VMEM(pos_bias.shape, f32),
        pltpu.VMEM((LANES, 8, two), f32),
        pltpu.VMEM((LANES, 8, two), f32),
        pltpu.VMEM((LANES, blocks, 16, two), bf16),
        pltpu.VMEM((LANES, blocks, two, block_len), bf16),
        pltpu.VMEM((spans, parts, 8, two), f32),
        pltpu.VMEM((parts, LANES, two, width), bf16),
        pltpu.VMEM((parts, LANES, two, width), bf16),
        pltpu.VMEM((parts, LANES, two, width), bf16),
        pltpu.VMEM((parts, LANES, two, width), bf16),
        pltpu.VMEM((parts, LANES, HEADS_PER_PART, two), f32),
        pltpu.VMEM((parts, LANES, HEADS_PER_PART, two), f32),
        pltpu.VMEM((SLOTS, 8, two), f32),
        pltpu.VMEM((parts, LANES, 2 * HEADS_PER_PART, two), f32),
        pltpu.VMEM((parts, LANES, 2 * HEADS_PER_PART, two), f32),
        pltpu.VMEM((3, LANES, 8, two), f32),
        pltpu.VMEM((3, HEADS_PER_PART, LANES, block_len, two), f32),
        pltpu.VMEM((HEADS_PER_PART, key_count, LANES * two), bf16),
        pltpu.VMEM((HEADS_PER_PART, key_count, LANES * two), bf16),
        pltpu.VMEM((LANES * two, key_count), bf16),
        pltpu.VMEM((parts, LANES, two, width), bf16),
        pltpu.VMEM((parts, LANES, two, width), bf16),
        pltpu.VMEM((SLOTS, rows, width), f32),
        pltpu.VMEM((parts, bias_rows // parts, block_len), f32),
        pltpu.VMEM((4, bias_rows // parts, block_len), f32),
        pltpu.VMEM((4, bias_rows // parts, block_len), f32),
        pltpu.VMEM((3, bias_rows // parts, block_len), f32),
        pltpu.VMEM((16, bias_rows // 128, block_len), f32),
        pltpu.VMEM((16, bias_rows // 128, block_len), f32),
        dma((6,)),
        dma((LANES,)),
        dma((LANES,)),
    ]
    scratch += [dma((parts, LANES)) for _ in range(10)]
    scratch += [dma((4,)), dma((4,)), dma((4,)), dma((3,)), dma((16,)), dma((16,))]
    pair_work = SLOTS * rows * key_count * feat
    call = pl.pallas_call(
        functools.partial(kernel, cfg),
        out_shape=(
            pltpu.VMEM((spans, rows, feat), bf16),
            pltpu.VMEM((key_count, feat), f32),
            pltpu.VMEM((key_count, feat), f32),
            pltpu.VMEM((bias_rows // 128, block_len), f32),
        ),
        in_specs=[smem, smem] + [anywhere] * 6,
        out_specs=(vmem, vmem, vmem, vmem),
        scratch_shapes=scratch,
        compiler_params=pltpu.CompilerParams(
            collective_id=0, has_side_effects=True, vmem_limit_bytes=46 * 2**20
        ),
        cost_estimate=pl.CostEstimate(
            flops=10 * pair_work, bytes_accessed=20 * 2**20, transcendentals=0
        ),
    )
    results = call(
        owner.T,
        slot.T,
        queries,
        outputs,
        out_grad,
        keys.reshape(key_count, feat),
        values.reshape(key_count, feat),
        pos_bias,
    )
    query_grad, key_grad, value_grad, bias_grad = pl.pallas_call(
        store,
        out_shape=tuple(jax.ShapeDtypeStruct(r.shape, r.dtype) for r in results),
        in_specs=[vmem] * 4,
        out_specs=(anywhere,) * 4,
        scratch_shapes=[dma((4,))],
        compiler_params=pltpu.CompilerParams(vmem_limit_bytes=2**20),
    )(*results)
    return (
        query_grad,
        key_grad.reshape(blocks, block_len, feat),
        value_grad.reshape(blocks, block_len, feat),
        bias_grad,
    )


def solution(mesh):
    rows = P(("dp", "seq"), None, None)
    pairs = P(("dp", "seq"), None)
    return jax.shard_map(
        per_device,
        mesh=mesh,
        in_specs=(rows, rows, rows, rows, rows, pairs, pairs, P()),
        out_specs=(rows, rows, rows, pairs),
        check_vma=False,
    )
```

```python
import functools

import jax
import jax.numpy as jnp
from jax import lax
from jax.experimental import pallas as pl
from jax.experimental.pallas import tpu as pltpu
from jax.sharding import PartitionSpec as P

REACH = 2
CAP = 2
LANES = 2 * REACH + 1
SLOTS = LANES * CAP
HEADS_PER_PART = 2
AHEAD = 1
FAR_AHEAD = 4
HELD = 1
UNUSED = 1e30
MESH = pl.DeviceIdType.MESH
REMOTE = tuple(lane for lane in range(LANES) if lane != REACH)
NEAR = (REACH - 1, REACH + 1)
FAR = (0, LANES - 1)


def rows_dot(a, b):
    return lax.dot_general(a, b, (((1,), (1,)), ((), ())), preferred_element_type=jnp.float32)


def plain_dot(a, b):
    return jnp.dot(a, b, preferred_element_type=jnp.float32)


def kernel(
    cfg,
    owner_ref,
    slot_ref,
    q_hbm,
    o_hbm,
    g_hbm,
    k_hbm,
    v_hbm,
    bias_hbm,
    qg_ref,
    kg_ref,
    vg_ref,
    bg_ref,
    q_ref,
    o_ref,
    g_ref,
    k_ref,
    v_ref,
    bias_ref,
    meta_send,
    meta_recv,
    mask_row,
    mask_col,
    terms,
    q_send,
    q_recv,
    g_send,
    g_recv,
    part_send,
    part_recv,
    part_pick,
    total_send,
    total_recv,
    tops,
    exps,
    w_wide,
    d_wide,
    d_tall,
    dq_send,
    dq_recv,
    dq_pick,
    bias_sum,
    core_recv,
    z_send,
    z_recv,
    xy_send,
    xy_recv,
    load_sem,
    meta_ss,
    meta_rs,
    q_ss,
    q_rs,
    g_ss,
    g_rs,
    part_ss,
    part_rs,
    total_ss,
    total_rs,
    dq_ss,
    dq_rs,
    core_ss,
    core_rs,
    z_ss,
    z_rs,
    xy_ss,
    xy_rs,
):
    spans, rows, seq_count, parts, blocks, scaling = cfg
    width = HEADS_PER_PART * 128
    pairs = 2 * spans
    dp = lax.axis_index("dp")
    me = lax.axis_index("seq")
    at_z, at_x, at_y = me // 16, (me // 4) % 4, me % 4

    def owner_at(lane):
        return (dp, lax.rem(me + (lane - REACH) + seq_count, seq_count))

    def asker_at(lane):
        return (dp, lax.rem(me - (lane - REACH) + seq_count, seq_count))

    def along_z(z):
        return (dp, z * 16 + at_x * 4 + at_y)

    def across(turn):
        return (dp, at_z * 16 + ((at_x + turn // 4) % 4) * 4 + (at_y + turn % 4) % 4)

    inputs = (
        (q_hbm, q_ref),
        (g_hbm, g_ref),
        (k_hbm, k_ref),
        (bias_hbm, bias_ref),
        (o_hbm, o_ref),
        (v_hbm, v_ref),
    )
    loads = [
        pltpu.make_async_copy(far, near, load_sem.at[n]) for n, (far, near) in enumerate(inputs)
    ]
    load_q, load_g, load_k, load_bias, load_o, load_v = loads
    greeted = [owner_at(lane) for lane in REMOTE] + [across(turn) for turn in range(1, 16)]
    greeted += [along_z((at_z + turn) % 4) for turn in (1, 2, 3)] + [(1 - dp, me)]
    barrier = pltpu.get_barrier_semaphore()
    for device in greeted:
        pl.semaphore_signal(barrier, inc=1, device_id=device, device_id_type=MESH)
    for load in loads:
        load.start()

    lane_of = [
        lax.rem(owner_ref[p % 2, p // 2] - me + REACH + seq_count, seq_count) for p in range(pairs)
    ]
    place = []
    for p in range(pairs):
        rank = jnp.int32(0)
        for other in range(p):
            rank = rank + jnp.where(lane_of[other] == lane_of[p], 1, 0)
        place.append(jnp.minimum(lane_of[p] * CAP + rank, SLOTS - 1))
    chosen, filled, block_id, partner = [], [], [], []
    for s in range(SLOTS):
        pick, used, block, mate = jnp.int32(0), jnp.int32(0), jnp.int32(0), jnp.int32(0)
        for p in range(pairs):
            hit = place[p] == s
            pick = jnp.where(hit, p // 2, pick)
            used = jnp.where(hit, 1, used)
            block = jnp.where(hit, slot_ref[p % 2, p // 2], block)
            mate = jnp.where(hit, place[p ^ 1], mate)
        chosen.append(pick)
        filled.append(used)
        block_id.append(block)
        partner.append((mate // 2) * 2 + (mate + s) % 2)

    lane_id = lax.broadcasted_iota(jnp.int32, (8, 128), 1)
    row_id = lax.broadcasted_iota(jnp.int32, (8, 128), 0)
    first_half = lane_id < rows

    def to_owner(held, landed, sent, got, at, lane):
        return pltpu.make_async_remote_copy(
            src_ref=held.at[at],
            dst_ref=landed.at[at],
            send_sem=sent.at[at],
            recv_sem=got.at[at],
            device_id=owner_at(lane),
            device_id_type=MESH,
        )

    def to_asker(held, landed, sent, got, at, lane):
        return pltpu.make_async_remote_copy(
            src_ref=held.at[at],
            dst_ref=landed.at[at],
            send_sem=sent.at[at],
            recv_sem=got.at[at],
            device_id=asker_at(lane),
            device_id_type=MESH,
        )

    def meta_copy(lane):
        return to_owner(meta_send, meta_recv, meta_ss, meta_rs, lane, lane)

    def q_copy(part, lane):
        return to_owner(q_send, q_recv, q_ss, q_rs, (part, lane), lane)

    def g_copy(part, lane):
        return to_owner(g_send, g_recv, g_ss, g_rs, (part, lane), lane)

    def part_copy(part, lane):
        return to_asker(part_send, part_recv, part_ss, part_rs, (part, lane), lane)

    def total_copy(part, lane):
        return to_owner(total_send, total_recv, total_ss, total_rs, (part, lane), lane)

    def dq_copy(part, lane):
        return to_asker(dq_send, dq_recv, dq_ss, dq_rs, (part, lane), lane)

    def core_copy(part):
        quarter = part % 4
        return pltpu.make_async_remote_copy(
            src_ref=bias_sum.at[part],
            dst_ref=core_recv.at[quarter],
            send_sem=core_ss.at[quarter],
            recv_sem=core_rs.at[quarter],
            device_id=(1 - dp, me),
            device_id_type=MESH,
        )

    def z_copy(quarter, turn):
        return pltpu.make_async_remote_copy(
            src_ref=z_send.at[quarter],
            dst_ref=z_recv.at[turn],
            send_sem=z_ss.at[quarter],
            recv_sem=z_rs.at[turn],
            device_id=along_z(quarter),
            device_id_type=MESH,
        )

    def xy_copy(turn):
        target = ((at_x + turn // 4) % 4) * 4 + (at_y + turn % 4) % 4
        return pltpu.make_async_remote_copy(
            src_ref=xy_send.at[target],
            dst_ref=xy_recv.at[turn],
            send_sem=xy_ss.at[turn],
            recv_sem=xy_rs.at[turn],
            device_id=across(turn),
            device_id_type=MESH,
        )

    def pack(part, source, held, landed, lanes):
        columns = pl.ds(pl.multiple_of(part * width, width), width)
        for lane in lanes:
            target = landed if lane == REACH else held
            for half in range(CAP):
                target[part, lane, half * rows : (half + 1) * rows, :] = source[
                    chosen[lane * CAP + half], :, columns
                ]

    def start(part, copy, lanes):
        for lane in lanes:
            if lane != REACH:
                copy(part, lane).start()

    def send_q(part, lanes):
        pack(part, q_ref, q_send, q_recv, lanes)
        start(part, q_copy, lanes)

    def send_g(part, lanes):
        pack(part, g_ref, g_send, g_recv, lanes)
        start(part, g_copy, lanes)

    for lane in range(LANES):
        tile = jnp.where(first_half, block_id[2 * lane], block_id[2 * lane + 1])
        target = meta_recv if lane == REACH else meta_send
        target[lane] = tile.astype(jnp.float32)
    part_pick[...] = jnp.zeros(part_pick.shape, jnp.float32)
    load_q.wait()
    for part in range(AHEAD):
        pack(part, q_ref, q_send, q_recv, range(LANES))
    pl.semaphore_wait(barrier, len(greeted))
    for lane in REMOTE:
        meta_copy(lane).start()
    for part in range(AHEAD):
        start(part, q_copy, FAR + NEAR)
    load_g.wait()

    def send_far(part, carry):
        @pl.when(part < parts)
        def _():
            send_q(part, FAR)

        send_g(part - AHEAD, FAR)
        return carry

    lax.fori_loop(AHEAD, AHEAD + FAR_AHEAD, send_far, 0)
    load_o.wait()

    def span_terms(span, carry):
        wide_lane = lax.broadcasted_iota(jnp.int32, (rows, 128), 1)
        gathered = jnp.zeros((rows, 128), jnp.float32)
        for head in range(parts * HEADS_PER_PART):
            cols = slice(head * 128, (head + 1) * 128)
            product = g_ref[span, :, cols].astype(jnp.float32) * o_ref[span, :, cols].astype(
                jnp.float32
            )
            gathered = jnp.where(
                wide_lane == head, jnp.sum(product, axis=1, keepdims=True), gathered
            )
        turned = jnp.concatenate([gathered, gathered], axis=0).T
        for part in range(parts):
            first = part * HEADS_PER_PART
            terms[span, part, HEADS_PER_PART : 2 * HEADS_PER_PART, :] = turned[
                first : first + HEADS_PER_PART, :
            ]
        return carry

    lax.fori_loop(0, spans, span_terms, 0)
    load_k.wait()
    load_bias.wait()
    load_v.wait()

    for lane in REMOTE:
        meta_copy(lane).wait_recv()
    for lane in range(LANES):
        wide = jnp.broadcast_to(meta_recv[lane, 0:1, :], (128, 128))
        tall = wide.T
        for b in range(blocks):
            mask_row[lane, b] = jnp.where(wide[0:16] == b, 1.0, 0.0).astype(jnp.bfloat16)
            mask_col[lane, b] = jnp.where(tall == b, 1.0, 0.0).astype(jnp.bfloat16)

    def picked(products, ids):
        result = products[0:128]
        for b in range(1, blocks):
            result = jnp.where(ids == b, products[b * 128 : (b + 1) * 128], result)
        return result

    def score(part):
        slot_now = lax.rem(part, 3)
        for lane in REMOTE:
            q_copy(part, lane).wait_recv()
        for sub in range(HEADS_PER_PART):
            cols = pl.ds(pl.multiple_of(part * width + sub * 128, 128), 128)
            inner = slice(sub * 128, (sub + 1) * 128)
            key_rows = k_ref[:, cols]
            bias_rows = bias_ref[
                pl.ds(pl.multiple_of((part * HEADS_PER_PART + sub) * rows, rows), rows), :
            ]
            bias_turned = jnp.concatenate([bias_rows, bias_rows], axis=0).T
            for lane in range(LANES):
                ids = meta_recv[lane, 0:1, :]
                scores = (
                    picked(rows_dot(key_rows, q_recv[part, lane, :, inner]), ids) * scaling
                    + bias_turned
                )
                top = jnp.max(scores, axis=0, keepdims=True)
                lifted = jnp.exp(scores - top)
                exps[slot_now, sub, lane] = lifted
                tops[slot_now, lane, sub : sub + 1, :] = top
                target = part_recv if lane == REACH else part_send
                target[part, lane, sub : sub + 1, :] = top + jnp.log(
                    jnp.sum(lifted, axis=0, keepdims=True)
                )
        for lane in REMOTE:
            part_copy(part, lane).start()

    def combine(part):
        for lane in REMOTE:
            part_copy(part, lane).wait_recv()
        for lane in range(LANES):
            part_pick[2 * lane, 0:HEADS_PER_PART, :] = part_recv[part, lane]
            part_pick[2 * lane + 1] = pltpu.roll(part_pick[2 * lane], rows, 1)
        for lane in range(LANES):
            s = 2 * lane
            mine = part_pick[s]
            mate = jnp.where(first_half, part_pick[partner[s]], part_pick[partner[s + 1]])
            top = jnp.maximum(mine, mate)
            total = top + jnp.log(jnp.exp(mine - top) + jnp.exp(mate - top))
            used = jnp.where(first_half, filled[s], filled[s + 1])
            total = jnp.where(used > 0, total, UNUSED)
            row = jnp.where(first_half, terms[chosen[s], part], terms[chosen[s + 1], part])
            target = total_recv if lane == REACH else total_send
            target[part, lane] = jnp.where(row_id < HEADS_PER_PART, total, row)[
                0 : 2 * HEADS_PER_PART
            ]
        for lane in REMOTE:
            total_copy(part, lane).start()

    def send_dq(part, carry):
        for lane in REMOTE:
            dq_copy(part, lane).start()
        return carry

    def gradients(part):
        slot_now = lax.rem(part, 3)
        for lane in REMOTE:
            total_copy(part, lane).wait_recv()
            g_copy(part, lane).wait_recv()

        @pl.when(part >= HELD + 1)
        def _():
            send_dq(part - HELD - 1, 0)

        @pl.when(part == parts - 1)
        def _():
            lax.fori_loop(parts - 1 - HELD, parts - 1, send_dq, 0)

        for sub in range(HEADS_PER_PART):
            cols = pl.ds(pl.multiple_of(part * width + sub * 128, 128), 128)
            inner = slice(sub * 128, (sub + 1) * 128)
            value_rows = v_ref[:, cols]
            bias_part = jnp.zeros((128, 128), jnp.float32)
            for lane in range(LANES):
                ids = meta_recv[lane, 0:1, :]
                grad_weights = picked(rows_dot(value_rows, g_recv[part, lane, :, inner]), ids)
                factor = jnp.exp(
                    tops[slot_now, lane, sub : sub + 1, :] - total_recv[part, lane, sub : sub + 1, :]
                )
                row = total_recv[part, lane, HEADS_PER_PART + sub : HEADS_PER_PART + sub + 1, :]
                weights = exps[slot_now, sub, lane] * factor
                grad_scores = weights * (grad_weights - row)
                bias_part = bias_part + grad_scores
                weights_low = weights.astype(jnp.bfloat16).reshape(8, 16, 128)
                grad_low = grad_scores.astype(jnp.bfloat16)
                grad_tall = grad_low.T
                grad_low = grad_low.reshape(8, 16, 128)
                beside = slice(lane * 128, (lane + 1) * 128)
                for b in range(blocks):
                    down = slice(b * 128, (b + 1) * 128)
                    mask = mask_row[lane, b][None]
                    w_wide[sub, down, beside] = (weights_low * mask).reshape(128, 128)
                    d_wide[sub, down, beside] = (grad_low * mask).reshape(128, 128)
                    d_tall[beside, down] = grad_tall * mask_col[lane, b]
            dq = (plain_dot(d_tall[...], k_ref[:, cols]) * scaling).astype(jnp.bfloat16)
            for lane in range(LANES):
                target = dq_recv if lane == REACH else dq_send
                target[part, lane, :, inner] = dq[lane * 128 : (lane + 1) * 128]
            bias_turned = bias_part.T
            bias_sum[part, sub * rows : (sub + 1) * rows, :] = (
                bias_turned[0:rows] + bias_turned[rows : 2 * rows]
            )
        @pl.when(part == parts - 1)
        def _():
            send_dq(part, 0)

        @pl.when(part // 4 != dp)
        def _():
            core_copy(part).start()

        for sub in range(HEADS_PER_PART):
            inner = slice(sub * 128, (sub + 1) * 128)
            queries = q_recv[part, :, :, inner].reshape(LANES * 128, 128)
            cotangents = g_recv[part, :, :, inner].reshape(LANES * 128, 128)
            cols = pl.ds(pl.multiple_of(part * width + sub * 128, 128), 128)
            kg_ref[:, cols] = plain_dot(d_wide[sub], queries) * scaling
            vg_ref[:, cols] = plain_dot(w_wide[sub], cotangents)

    def reduce_cores(part):
        quarter = part % 4

        @pl.when(part // 4 == dp)
        def _():
            core_copy(part).wait_recv()
            z_send[quarter] = bias_sum[part] + core_recv[quarter]

            @pl.when(quarter != at_z)
            def _():
                z_copy(quarter, (at_z - quarter + 4) % 4 - 1).start()

    def gather(part, carry):
        columns = pl.ds(pl.multiple_of(part * width, width), width)
        for lane in REMOTE:
            dq_copy(part, lane).wait_recv()
        for lane in range(LANES):
            for half in range(CAP):
                dq_pick[lane * CAP + half] = dq_recv[
                    part, lane, half * rows : (half + 1) * rows, :
                ].astype(jnp.float32)
        for span in range(spans):
            both = dq_pick[place[2 * span]] + dq_pick[place[2 * span + 1]]
            qg_ref[span, :, columns] = both.astype(jnp.bfloat16)
        return carry

    def step(t, carry):
        @pl.when(t + FAR_AHEAD < parts)
        def _():
            send_far(t + FAR_AHEAD + AHEAD, 0)

        @pl.when(t + AHEAD < parts)
        def _():
            send_q(t + AHEAD, NEAR + (REACH,))

        @pl.when(t < parts)
        def _():
            send_g(t, NEAR + (REACH,))
            score(t)

        @pl.when((t >= 1) & (t < parts + 1))
        def _():
            combine(t - 1)

        @pl.when(t >= 2)
        def _():
            gradients(t - 2)

        @pl.when(t >= 3)
        def _():
            reduce_cores(t - 3)

        @pl.when(t >= HELD + 4)
        def _():
            gather(t - HELD - 4, 0)

        return carry

    lax.fori_loop(0, parts + 2, step, 0)

    reduce_cores(parts - 1)
    for turn in range(3):
        z_copy(at_z, turn).wait_recv()
    mine = z_send[at_z] + z_recv[0] + z_recv[1] + z_recv[2]
    xy_send[...] = mine.reshape(16, 8, 128)
    for turn in range(1, 16):
        xy_copy(turn).start()
    lax.fori_loop(parts - HELD - 2, parts, gather, 0)
    for turn in range(1, 16):
        xy_copy(turn).wait_recv()
    total = xy_send[at_x * 4 + at_y]
    for turn in range(1, 16):
        total = total + xy_recv[turn]
    bg_ref[...] = total
    for turn in range(1, 16):
        xy_copy(turn).wait_send()
    for lane in REMOTE:
        meta_copy(lane).wait_send()

    def finish(part, carry):
        for lane in REMOTE:
            q_copy(part, lane).wait_send()
            g_copy(part, lane).wait_send()
            part_copy(part, lane).wait_send()
            total_copy(part, lane).wait_send()
            dq_copy(part, lane).wait_send()

        @pl.when(part // 4 != dp)
        def _():
            core_copy(part).wait_send()

        @pl.when((part // 4 == dp) & (part % 4 != at_z))
        def _():
            z_copy(part % 4, (at_z - part % 4 + 4) % 4 - 1).wait_send()

        return carry

    lax.fori_loop(0, parts, finish, 0)


def store(*refs):
    sem = refs[8]
    copies = [pltpu.make_async_copy(refs[n], refs[4 + n], sem.at[n]) for n in range(4)]
    for copy in copies:
        copy.start()
    for copy in copies:
        copy.wait()


def per_device(queries, outputs, out_grad, keys, values, owner, slot, pos_bias):
    spans, rows, feat = queries.shape
    blocks, block_len, _ = keys.shape
    heads = pos_bias.shape[0] // rows
    head_size = feat // heads
    parts = heads // HEADS_PER_PART
    width = HEADS_PER_PART * head_size
    seq_count = lax.axis_size("seq")
    key_count = blocks * block_len
    cfg = (spans, rows, seq_count, parts, blocks, head_size ** (-0.5))
    vmem = pl.BlockSpec(memory_space=pltpu.VMEM)
    smem = pl.BlockSpec(memory_space=pltpu.SMEM)
    anywhere = pl.BlockSpec(memory_space=pl.ANY)
    f32, bf16 = jnp.float32, jnp.bfloat16
    two = CAP * rows
    bias_rows = heads * rows
    dma = pltpu.SemaphoreType.DMA
    near = [queries, outputs, out_grad]
    scratch = [pltpu.VMEM(array.shape, array.dtype) for array in near]
    scratch += [
        pltpu.VMEM((key_count, feat), bf16),
        pltpu.VMEM((key_count, feat), bf16),
        pltpu.VMEM(pos_bias.shape, f32),
        pltpu.VMEM((LANES, 8, two), f32),
        pltpu.VMEM((LANES, 8, two), f32),
        pltpu.VMEM((LANES, blocks, 16, two), bf16),
        pltpu.VMEM((LANES, blocks, two, block_len), bf16),
        pltpu.VMEM((spans, parts, 8, two), f32),
        pltpu.VMEM((parts, LANES, two, width), bf16),
        pltpu.VMEM((parts, LANES, two, width), bf16),
        pltpu.VMEM((parts, LANES, two, width), bf16),
        pltpu.VMEM((parts, LANES, two, width), bf16),
        pltpu.VMEM((parts, LANES, HEADS_PER_PART, two), f32),
        pltpu.VMEM((parts, LANES, HEADS_PER_PART, two), f32),
        pltpu.VMEM((SLOTS, 8, two), f32),
        pltpu.VMEM((parts, LANES, 2 * HEADS_PER_PART, two), f32),
        pltpu.VMEM((parts, LANES, 2 * HEADS_PER_PART, two), f32),
        pltpu.VMEM((3, LANES, 8, two), f32),
        pltpu.VMEM((3, HEADS_PER_PART, LANES, block_len, two), f32),
        pltpu.VMEM((HEADS_PER_PART, key_count, LANES * two), bf16),
        pltpu.VMEM((HEADS_PER_PART, key_count, LANES * two), bf16),
        pltpu.VMEM((LANES * two, key_count), bf16),
        pltpu.VMEM((parts, LANES, two, width), bf16),
        pltpu.VMEM((parts, LANES, two, width), bf16),
        pltpu.VMEM((SLOTS, rows, width), f32),
        pltpu.VMEM((parts, bias_rows // parts, block_len), f32),
        pltpu.VMEM((4, bias_rows // parts, block_len), f32),
        pltpu.VMEM((4, bias_rows // parts, block_len), f32),
        pltpu.VMEM((3, bias_rows // parts, block_len), f32),
        pltpu.VMEM((16, bias_rows // 128, block_len), f32),
        pltpu.VMEM((16, bias_rows // 128, block_len), f32),
        dma((6,)),
        dma((LANES,)),
        dma((LANES,)),
    ]
    scratch += [dma((parts, LANES)) for _ in range(10)]
    scratch += [dma((4,)), dma((4,)), dma((4,)), dma((3,)), dma((16,)), dma((16,))]
    pair_work = SLOTS * rows * key_count * feat
    call = pl.pallas_call(
        functools.partial(kernel, cfg),
        out_shape=(
            pltpu.VMEM((spans, rows, feat), bf16),
            pltpu.VMEM((key_count, feat), f32),
            pltpu.VMEM((key_count, feat), f32),
            pltpu.VMEM((bias_rows // 128, block_len), f32),
        ),
        in_specs=[smem, smem] + [anywhere] * 6,
        out_specs=(vmem, vmem, vmem, vmem),
        scratch_shapes=scratch,
        compiler_params=pltpu.CompilerParams(
            collective_id=0, has_side_effects=True, vmem_limit_bytes=46 * 2**20
        ),
        cost_estimate=pl.CostEstimate(
            flops=10 * pair_work, bytes_accessed=20 * 2**20, transcendentals=0
        ),
    )
    results = call(
        owner.T,
        slot.T,
        queries,
        outputs,
        out_grad,
        keys.reshape(key_count, feat),
        values.reshape(key_count, feat),
        pos_bias,
    )
    query_grad, key_grad, value_grad, bias_grad = pl.pallas_call(
        store,
        out_shape=tuple(jax.ShapeDtypeStruct(r.shape, r.dtype) for r in results),
        in_specs=[vmem] * 4,
        out_specs=(anywhere,) * 4,
        scratch_shapes=[dma((4,))],
        compiler_params=pltpu.CompilerParams(vmem_limit_bytes=2**20),
    )(*results)
    return (
        query_grad,
        key_grad.reshape(blocks, block_len, feat),
        value_grad.reshape(blocks, block_len, feat),
        bias_grad,
    )


def solution(mesh):
    rows = P(("dp", "seq"), None, None)
    pairs = P(("dp", "seq"), None)
    return jax.shard_map(
        per_device,
        mesh=mesh,
        in_specs=(rows, rows, rows, rows, rows, pairs, pairs, P()),
        out_specs=(rows, rows, rows, pairs),
        check_vma=False,
    )
```
